128 devices in a mesh: branch: 32 (over x, z, core), sub: 4 (over y).
Axes of the slice: x: 4, y: 4, z: 4, core: 2. Of those that a mesh axis runs over, the one named last changes fastest.
Arguments:
- right_sides: bfloat16 [32, 786432], P(None, ('branch', 'sub')), may hold values from -6 to 6
- near_blocks: bfloat16 [3072, 6, 256, 256], P(('branch', 'sub')), may hold values from -0.15625 to 0.15625
- near_list: int32 [3072, 6], P(('branch', 'sub')), may hold values from -1 to 3071, as said below
- leaf_basis: bfloat16 [3072, 64, 256], P(('branch', 'sub')), may hold values from -0.375 to 0.375
- leaf_parent: int32 [128, 24], P(('branch', 'sub')), may hold values from 0 to 5, never falling along the last dimension, each value on 1 to 6 neighbouring positions
- leaf_upward_matrix: float32 [3072, 64, 64], P(('branch', 'sub')), may hold values from -0.375 to 0.375
- mid_pairs: int32 [768, 4], P(('branch', 'sub')), may hold values from -1 to 767, as said below
- mid_coupling: float32 [768, 4, 64, 64], P(('branch', 'sub')), may hold values from -0.75 to 0.75
- mid_transfer: float32 [768, 64, 64], P(('branch', 'sub')), may hold values from -0.3125 to 0.3125
- node_pairs: int32 [128, 8], P('branch'), may hold values from -1 to 127, as said below
- node_coupling: float32 [128, 8, 64, 64], P('branch'), may hold values from -0.5 to 0.5
- node_transfer: float32 [128, 64, 64], P('branch'), may hold values from -0.375 to 0.375
- branch_pairs: int32 [32, 4], P('branch'), may hold values from -1 to 31, as said below
- branch_coupling: float32 [32, 4, 64, 64], P('branch'), may hold values from -1.5 to 1.5
Outputs:
- product: float32 [32, 786432], P(None, ('branch', 'sub'))
The draws below stay inside these ranges and needn't reach their ends.
Inputs may be any that keep to these rules, and one draw needn't show every extreme that they name: `near_list`: entry (l, 0) is l itself; every other entry is -1 or a leaf j != l with |j - l| <= 24; the leaves of a row are distinct. `leaf_parent`: within a row the parent never falls, and every parent has 1 to 6 leaves. `mid_pairs`: every entry is -1 or a level-1 cluster j != q with |j - q| <= 6; the clusters of a row are distinct. `node_pairs`: every entry is -1 or a node other than the row's own; the nodes of a row are distinct; entry (p, 0) is never -1. `branch_pairs`: every entry is -1 or a branch other than the row's own; the branches of a row are distinct; entry (b, 0) is never -1.
All inputs are finite; a program needn't handle non-finite values.
Results may differ from the reference program's by a relative error of at most 0.0003.
Values may be sent and summed in bfloat16 or wider, within the bound.
A program may use at most 128 MiB of HBM per device.

```python
import math
import jax
import jax.numpy as jnp
import numpy as np
from jax import lax

LEAF = 256
RANK = 64
NRHS = 32
LPD = 24
NEAR = 6
FAR1 = 4
FAR2 = 8
FAR3 = 4
C1 = 6
BRANCHES = 32
SUBS = 4
NODES = 128
LEAVES = 3072
L1 = 768
POINTS = 786432


def offsets(base_key, row_count, reach_size, pick_count):
    scores = jax.random.randint(base_key, (row_count, 2 * reach_size), 0, 1 << 20)
    scores = scores * (2 * reach_size) + jnp.arange(2 * reach_size, dtype=jnp.int32)[None, :]
    ranked = jnp.argsort(scores, axis=1)[:, :pick_count].astype(jnp.int32)
    return jnp.where(ranked < reach_size, ranked - reach_size, ranked - reach_size + 1)


def partners(base_key, row_count, pick_count):
    scores = jax.random.randint(base_key, (row_count, row_count), 0, 1 << 16)
    scores = scores * row_count + jnp.arange(row_count, dtype=jnp.int32)[None, :]
    scores = jnp.where(jnp.eye(row_count, dtype=bool), jnp.int32(1 << 30), scores)
    return jnp.argsort(scores, axis=1)[:, :pick_count].astype(jnp.int32)


def force_first(result, row_at, value):
    row_values = result[row_at]
    row_values = jnp.where(row_values == value, -1, row_values)
    row_values = row_values.at[0].set(value)
    return result.at[row_at].set(row_values)


def draw_near_list(key, part):
    key = jax.random.fold_in(key, 11)
    key_pick, key_rate, key_roll = jax.random.split(key, 3)
    leaf_ids = jnp.arange(LEAVES, dtype=jnp.int32)[:, None]
    target = leaf_ids + offsets(key_pick, LEAVES, LPD, NEAR - 1)
    drop_rate = jnp.repeat(jax.random.randint(key_rate, (NODES,), 0, 5), LPD)[:, None]
    rolled = jax.random.randint(key_roll, (LEAVES, NEAR - 1), 0, 8)
    keep_mask = (rolled >= drop_rate) & (target >= 0) & (target < LEAVES)
    result = jnp.concatenate([leaf_ids, jnp.where(keep_mask, target, -1)], axis=1)
    return result.at[0, NEAR - 1].set(-1).astype(jnp.int32)


def draw_mid_pairs(key, part):
    key = jax.random.fold_in(key, 12)
    key_pick, key_roll = jax.random.split(key, 2)
    cluster_ids = jnp.arange(L1, dtype=jnp.int32)[:, None]
    target = cluster_ids + offsets(key_pick, L1, C1, FAR1)
    rolled = jax.random.randint(key_roll, (L1, FAR1), 0, 8)
    keep_mask = (rolled >= 2) & (target >= 0) & (target < L1)
    result = jnp.where(keep_mask, target, -1)
    result = result.at[0, FAR1 - 1].set(-1)
    return force_first(result, L1 - 2, L1 - 1).astype(jnp.int32)


def draw_node_pairs(key, part):
    key = jax.random.fold_in(key, 13)
    key_pick, key_roll = jax.random.split(key, 2)
    target = partners(key_pick, NODES, FAR2)
    rolled = jax.random.randint(key_roll, (NODES, FAR2), 0, 8)
    slot_ids = jnp.arange(FAR2, dtype=jnp.int32)[None, :]
    result = jnp.where((rolled >= 2) | (slot_ids == 0), target, -1)
    result = result.at[0, FAR2 - 1].set(-1)
    return force_first(result, 0, NODES - 1).astype(jnp.int32)


def draw_branch_pairs(key, part):
    key = jax.random.fold_in(key, 14)
    key_pick, key_roll = jax.random.split(key, 2)
    target = partners(key_pick, BRANCHES, FAR3)
    rolled = jax.random.randint(key_roll, (BRANCHES, FAR3), 0, 8)
    slot_ids = jnp.arange(FAR3, dtype=jnp.int32)[None, :]
    result = jnp.where((rolled >= 2) | (slot_ids == 0), target, -1)
    result = result.at[0, FAR3 - 1].set(-1)
    return force_first(result, 0, BRANCHES - 1).astype(jnp.int32)


def block_levels(own_key, dims, shards, low, high):
    factor_of = 1.0
    for position, blocks in shards:
        steps = jax.random.uniform(jax.random.fold_in(jax.random.fold_in(own_key, 6), position), (blocks,), jnp.float32, low / len(shards), high / len(shards))
        factor_of = factor_of * jnp.repeat(jnp.exp(steps), dims[position] // blocks).reshape((-1,) + (1,) * (len(dims) - 1 - position))
    return factor_of


def length_profile(count, total, most, lean):
    loads = [(1 << 20) // math.isqrt(grade ** lean) + 1 for grade in range(2, count + 1)]
    spare, counts = total - most - (count - 1), [1] * (count - 1)
    while spare > 0:
        movable = [i for i in range(count - 1) if counts[i] < most]
        pool, remaining = sum([loads[i] for i in movable]), spare
        for i in movable:
            more = min(most - counts[i], max(1, remaining * loads[i] // pool), spare)
            counts[i] = counts[i] + more
            spare = spare - more
    return np.array([most] + counts)


def uneven(own_key, number_of, total, most, lean):
    if number_of == 2:
        one = jax.random.randint(own_key, (), max(1, total - most), min(most, total - 1) + 1)
        return jnp.stack([one, total - one])
    lengths = jnp.asarray(length_profile(number_of, total, most, lean), jnp.int32)
    twos = (number_of - 1) // 2
    giver, receiver = lengths[1:1 + 2 * twos:2], lengths[2:2 + 2 * twos:2]
    margin = jnp.minimum(giver - 1, most - receiver)
    passed = jax.random.randint(jax.random.fold_in(own_key, 1), (twos,), 0, 1 << 20) % (margin + 1)
    lengths = lengths.at[1:1 + 2 * twos:2].set(giver - passed).at[2:2 + 2 * twos:2].set(receiver + passed)
    return lengths[jax.random.permutation(jax.random.fold_in(own_key, 2), number_of)]


def noise(stream_key, shape, spread, limit, cuts=(), held_as=jnp.bfloat16):
    drawn = spread * jax.random.normal(stream_key, shape, jnp.float32)
    if cuts:
        drawn = drawn * block_levels(stream_key, shape, cuts, -0.22, 0.18)
    return jnp.clip(drawn, -limit, limit).astype(held_as)


def setup_inputs(seed: int = 0) -> dict:
    key_list = jax.random.split(jax.random.key(seed), 15)
    return {
        "right_sides": noise(key_list[0], (NRHS, POINTS), 1.0, 6.0, ((1, 128),)),
        "near_blocks": noise(key_list[1], (LEAVES, NEAR, LEAF, LEAF), (LEAF * NEAR) ** -0.5, 0.15625, ((0, 128),)),
        "near_list": draw_near_list(jax.random.fold_in(key_list[14], 71), 0),
        "leaf_basis": noise(key_list[3], (LEAVES, RANK, LEAF), LEAF ** -0.5, 0.375, ((0, 128),)),
        "leaf_parent": jax.vmap(lambda own: jnp.searchsorted(jnp.cumsum(uneven(own, C1, LPD, 6, 1)), jnp.arange(LPD), side="right"))(jax.random.split(key_list[4], NODES)).reshape((NODES, LPD)).astype(jnp.int32),
        "leaf_upward_matrix": noise(key_list[5], (LEAVES, RANK, RANK), (RANK * 4) ** -0.5, 0.375, ((0, 128),), jnp.float32),
        "mid_pairs": draw_mid_pairs(jax.random.fold_in(key_list[14], 71), 0),
        "mid_coupling": noise(key_list[7], (L1, FAR1, RANK, RANK), (RANK * FAR1 // 4) ** -0.5, 0.75, ((0, 128),), jnp.float32),
        "mid_transfer": noise(key_list[8], (L1, RANK, RANK), (RANK * C1) ** -0.5, 0.3125, ((0, 128),), jnp.float32),
        "node_pairs": draw_node_pairs(jax.random.fold_in(key_list[14], 71), 0),
        "node_coupling": noise(key_list[10], (NODES, FAR2, RANK, RANK), (RANK * FAR2 // 4) ** -0.5, 0.5, ((0, 32),), jnp.float32),
        "node_transfer": noise(key_list[11], (NODES, RANK, RANK), (RANK * SUBS) ** -0.5, 0.375, ((0, 32),), jnp.float32),
        "branch_pairs": draw_branch_pairs(jax.random.fold_in(key_list[14], 71), 0),
        "branch_coupling": noise(key_list[13], (BRANCHES, FAR3, RANK, RANK), (RANK * FAR3 // 16) ** -0.5, 1.5, ((0, 32),), jnp.float32),
    }


highest_accuracy = lax.Precision.HIGHEST


def masked_rows(source, indices):
    present = indices >= 0
    clipped = jnp.where(present, indices, 0).astype(jnp.int32)
    taken = source[clipped]
    out_shape = present.shape + (1,) * (taken.ndim - present.ndim)
    return jnp.where(present.reshape(out_shape), taken, jnp.zeros((), taken.dtype))


def reference(right_sides, near_blocks, near_list, leaf_basis, leaf_parent, leaf_upward_matrix, mid_pairs, mid_coupling, mid_transfer, node_pairs, node_coupling, node_transfer, branch_pairs, branch_coupling):
    leaves = right_sides.reshape(NRHS, LEAVES, LEAF).astype(jnp.float32)
    basis_full = leaf_basis.astype(jnp.float32)
    leaf_coefficients = jnp.einsum('nlk,lrk->lnr', leaves, basis_full, precision=highest_accuracy)
    parent_cluster = (leaf_parent + (jnp.arange(NODES, dtype=jnp.int32) * C1)[:, None]).reshape(LEAVES).astype(jnp.int32)
    raised_coefficients = jnp.einsum('xvm,xmu->xvu', leaf_coefficients, leaf_upward_matrix, precision=highest_accuracy)
    coef_mid = jax.ops.segment_sum(raised_coefficients, parent_cluster, num_segments=L1)
    coef_node = jnp.einsum('qns,qsr->qnr', coef_mid, mid_transfer, precision=highest_accuracy).reshape(NODES, C1, NRHS, RANK).sum(axis=1)
    top_terms = jnp.einsum('pns,psr->pnr', coef_node, node_transfer, precision=highest_accuracy)
    coef_branch = top_terms.reshape(BRANCHES, SUBS, NRHS, RANK).sum(axis=1)
    field_branch = jnp.einsum('bkrs,bkns->bnr', branch_coupling, masked_rows(coef_branch, branch_pairs), precision=highest_accuracy)
    field_node = jnp.einsum('pkrs,pkns->pnr', node_coupling, masked_rows(coef_node, node_pairs), precision=highest_accuracy)
    field_node = field_node + jnp.einsum('psr,pnr->pns', node_transfer, jnp.repeat(field_branch, SUBS, axis=0), precision=highest_accuracy)
    middle_potential = jnp.einsum('qkrs,qkns->qnr', mid_coupling, masked_rows(coef_mid, mid_pairs), precision=highest_accuracy)
    middle_potential = middle_potential + jnp.einsum('qsr,qnr->qns', mid_transfer, jnp.repeat(field_node, C1, axis=0), precision=highest_accuracy)
    leaf_potential = jnp.einsum('vpt,vct->vcp', leaf_upward_matrix, middle_potential[parent_cluster], precision=highest_accuracy)
    far_part = jnp.einsum('lrk,lnr->nlk', basis_full, leaf_potential, precision=highest_accuracy)
    node_blocks = near_blocks.reshape(NODES, LPD, NEAR, LEAF, LEAF)
    near_lists = near_list.reshape(NODES, LPD, NEAR)
    source = jnp.transpose(leaves, (1, 0, 2))

    def one_node(node_item):
        blocks, node_list = node_item
        picked = masked_rows(source, node_list)
        return jnp.einsum('ikab,iknb->nia', blocks.astype(jnp.float32), picked, precision=highest_accuracy)

    near_part = lax.map(one_node, (node_blocks, near_lists))
    near_part = jnp.transpose(near_part, (1, 0, 2, 3)).reshape(NRHS, LEAVES, LEAF)
    return (near_part + far_part).reshape(NRHS, POINTS)
```

```python
import jax
import jax.numpy as jnp
from jax import lax
from jax.experimental import pallas as pl
from jax.experimental.pallas import tpu as pltpu
from jax.sharding import PartitionSpec as P

MESH = pl.DeviceIdType.MESH
f32, bf16 = jnp.float32, jnp.bfloat16
RHS, LEAF, RANK, LEAVES, NEAR, MIDS = 32, 256, 64, 24, 6, 6
COLS = LEAVES * LEAF
PARTS = 4
ITEMS = 10


def nn(x, w):
    return lax.dot_general(x, w, (((1,), (0,)), ((), ())), preferred_element_type=f32)


def nt(x, w):
    return lax.dot_general(x, w, (((1,), (1,)), ((), ())), preferred_element_type=f32)


def split(value):
    high = value.astype(bf16).astype(f32)
    lane = lax.broadcasted_iota(jnp.int32, value.shape, 1)
    return jnp.where(lane < RANK, high, value - high).astype(bf16)


def halves(w):
    both = jnp.concatenate([w, w], axis=1)
    high = both.astype(bf16)
    return high, (both - high.astype(f32)).astype(bf16)


def twice(x):
    return jnp.concatenate([x, x], axis=1)


def apply_nn(x, pair):
    high, low = pair[:, :128], pair[:, 128:]
    return nn(twice(x), jnp.concatenate([high, high, low, low], axis=0))


def apply_nt(x, pair):
    return nt(twice(x), jnp.concatenate([pair, pair], axis=0))


def place_of(partner, base, empty):
    absent = -jnp.minimum(partner, 0)
    at = (partner - base) * (1 - absent) + empty * absent
    return jnp.minimum(jnp.maximum(at, 0), empty)


def kernel(
    near_list, leaf_parent, mid_pairs, node_pairs, branch_pairs,
    rhs, blocks, basis, upward, mid_coupling, mid_transfer, node_coupling, node_transfer,
    branch_coupling, out,
    rhs_buf, window, block_buf, basis_buf, up_raw, mid_coupling_raw, mid_transfer_raw, node_coupling_raw,
    transfer_raw, branch_coupling_raw, up_pair, mid_transfer_pair, raised, mid_window, mid_field,
    column, gather_a, gather_b, total,
    load_sem, block_sem, halo_send, halo_recv, mid_send, mid_recv, transfer_send, transfer_recv,
    column_send, column_recv, line_send, line_recv, plane_send, plane_recv, out_sem,
):
    b, s = lax.axis_index("branch"), lax.axis_index("sub")
    core, z, x = b % 2, (b // 2) % 4, b // 8
    me = b * 4 + s
    place = core * 4 + s

    def device(at):
        return (at // 4, at % 4)

    right, left = device((me + 1) % 128), device((me + 127) % 128)
    column_peers = []
    for d in range(1, 8):
        at = (place + d) % 8
        column_peers.append((x * 8 + z * 2 + at // 4, at % 4))
    x_peers = [(((x + d) % 4) * 8 + z * 2 + core, s) for d in (1, 2, 3)]
    z_peers = [(x * 8 + ((z + d) % 4) * 2 + core, s) for d in (1, 2, 3)]
    other_core = (x * 8 + z * 2 + 1 - core, s)
    peers = [right, left] + column_peers + x_peers + z_peers

    barrier = pltpu.get_barrier_semaphore()
    for peer in peers:
        pl.semaphore_signal(barrier, inc=1, device_id=peer, device_id_type=MESH)

    def send(src, dst, send_sem, recv_sem, peer):
        copy = pltpu.make_async_remote_copy(
            src_ref=src, dst_ref=dst, send_sem=send_sem, recv_sem=recv_sem,
            device_id=peer, device_id_type=MESH,
        )
        copy.start()
        return copy

    loads = [
        pltpu.make_async_copy(src, dst, load_sem.at[i])
        for i, (src, dst) in enumerate([
            (rhs, rhs_buf),
            (basis, basis_buf),
            (upward, up_raw),
            (mid_transfer, mid_transfer_raw),
            (node_transfer, transfer_raw.at[core]),
            (mid_coupling, mid_coupling_raw),
            (node_coupling.at[s], node_coupling_raw),
            (branch_coupling.at[0], branch_coupling_raw),
        ])
    ]
    per = LEAVES // PARTS
    block_loads = [
        pltpu.make_async_copy(
            blocks.at[pl.ds(i * per, per)], block_buf.at[pl.ds(i * per, per)], block_sem.at[i]
        )
        for i in range(PARTS)
    ]
    for copy in loads + block_loads:
        copy.start()
    window[3 * LEAVES] = jnp.zeros((RHS, LEAF), bf16)
    mid_window[3 * MIDS] = jnp.zeros((RHS, 128), bf16)
    raised[LEAVES] = jnp.zeros((RHS, 128), f32)
    gather_a[16] = jnp.zeros((ITEMS, 16, 128), bf16)
    gather_b[16] = jnp.zeros((ITEMS, 16, 128), bf16)

    def columns_of(leaf):
        return pl.ds(pl.multiple_of(leaf * LEAF, LEAF), LEAF)

    for copy in loads[:3]:
        copy.wait()

    @pl.loop(0, LEAVES // 6)
    def _(step):
        for i in range(6):
            leaf = step * 6 + i
            own = basis_buf[leaf]
            values = rhs_buf[:, columns_of(leaf)]
            window[LEAVES + leaf] = values
            coef = nt(values, jnp.concatenate([own, own], axis=0))
            pair = jnp.concatenate(halves(up_raw[leaf]), axis=1)
            up_pair[leaf] = pair
            raised[leaf] = apply_nn(split(coef), pair)

    parents = [leaf_parent[0, leaf] for leaf in range(LEAVES)]
    ends = [0]
    for q in range(1, MIDS):
        below = 0
        for parent in parents:
            below = below + jnp.minimum(jnp.maximum(q - parent, 0), 1)
        ends.append(below)
    ends.append(LEAVES)
    mids = []
    for q in range(MIDS):
        value = raised[ends[q]]
        for i in range(1, 6):
            leaf = ends[q] + i
            past = jnp.minimum(jnp.maximum(leaf + 1 - ends[q + 1], 0), 1)
            value = value + raised[leaf * (1 - past) + LEAVES * past]
        mids.append(value)
    loads[3].wait()
    node = jnp.zeros((RHS, 128), f32)
    for q in range(MIDS):
        pair = jnp.concatenate(halves(mid_transfer_raw[q]), axis=1)
        mid_transfer_pair[q] = pair
        coef = split(mids[q])
        mid_window[MIDS + q] = coef
        node = node + apply_nn(coef, pair)
    column[place] = split(node)

    pl.semaphore_wait(barrier, len(peers))
    sends = []
    loads[4].wait()
    sends.append(
        send(transfer_raw.at[core], transfer_raw.at[core], transfer_send, transfer_recv, other_core)
    )
    to_column = [
        send(column.at[place], column.at[place], column_send.at[d], column_recv.at[d], peer)
        for d, peer in enumerate(column_peers)
    ]
    own_mids = mid_window.at[pl.ds(MIDS, MIDS)]
    to_mids = [
        send(own_mids, mid_window.at[pl.ds(0, MIDS)], mid_send.at[0], mid_recv.at[0], right),
        send(own_mids, mid_window.at[pl.ds(2 * MIDS, MIDS)], mid_send.at[1], mid_recv.at[1], left),
    ]
    to_halo = []
    for i in range(PARTS):
        j = PARTS - 1 - i
        to_halo.append(
            send(window.at[pl.ds(LEAVES + j * per, per)], window.at[pl.ds(j * per, per)],
                 halo_send.at[0, j], halo_recv.at[0, j], right)
        )
        to_halo.append(
            send(window.at[pl.ds(LEAVES + i * per, per)],
                 window.at[pl.ds(2 * LEAVES + i * per, per)],
                 halo_send.at[1, i], halo_recv.at[1, i], left)
        )

    for part in range(PARTS):
        block_loads[part].wait()

        @pl.loop(0, per // 3)
        def _(step):
            for i in range(3):
                leaf = part * per + step * 3 + i
                total[:, columns_of(leaf)] = nt(
                    rhs_buf[:, columns_of(leaf)], block_buf[leaf, 0]
                )

    for copy in loads[5:]:
        copy.wait()

    sends[0].wait_recv()
    for copy in to_column:
        copy.wait_recv()
    for half in range(2):
        top = jnp.zeros((RHS, 128), f32)
        for sub in range(4):
            pair = jnp.concatenate(halves(transfer_raw[half, sub]), axis=1)
            top = top + apply_nn(column[half * 4 + sub], pair)
        top = split(top)
        gather_a[z * 4 + x, 8 + half] = top[:16]
        gather_b[x * 4 + z, 8 + half] = top[16:]
    for item in range(8):
        value = column[item]
        gather_a[z * 4 + x, item] = value[:16]
        gather_b[x * 4 + z, item] = value[16:]
    to_lines = [
        send(gather_a.at[z * 4 + x], gather_a.at[z * 4 + x], line_send.at[0, d], line_recv.at[0, d], peer)
        for d, peer in enumerate(x_peers)
    ] + [
        send(gather_b.at[x * 4 + z], gather_b.at[x * 4 + z], line_send.at[1, d], line_recv.at[1, d], peer)
        for d, peer in enumerate(z_peers)
    ]

    for copy in to_mids:
        copy.wait_recv()

    @pl.loop(0, MIDS)
    def _(q):
        field = jnp.zeros((RHS, 128), f32)
        for k in range(4):
            at = place_of(mid_pairs[k, q], me * MIDS - MIDS, 3 * MIDS)
            pair = jnp.concatenate(halves(mid_coupling_raw[q, k]), axis=1)
            field = field + apply_nt(mid_window[at], pair)
        mid_field[q] = field

    for copy in to_lines:
        copy.wait_recv()
    to_planes = [
        send(gather_a.at[pl.ds(z * 4, 4)], gather_a.at[pl.ds(z * 4, 4)], plane_send.at[0, d], plane_recv.at[0, d], peer)
        for d, peer in enumerate(z_peers)
    ] + [
        send(gather_b.at[pl.ds(x * 4, 4)], gather_b.at[pl.ds(x * 4, 4)], plane_send.at[1, d], plane_recv.at[1, d], peer)
        for d, peer in enumerate(x_peers)
    ]

    for copy in to_halo:
        copy.wait_recv()

    @pl.loop(0, LEAVES // 4)
    def _(step):
        for i in range(4):
            leaf = step * 4 + i
            value = total[:, columns_of(leaf)]
            for k in range(1, NEAR):
                at = place_of(near_list[k, leaf], me * LEAVES - LEAVES, 3 * LEAVES)
                value = value + nt(window[at], block_buf[leaf, k])
            total[:, columns_of(leaf)] = value

    for copy in to_planes:
        copy.wait_recv()

    def gathered(partner, branch, item):
        at_x, at_z = branch >> 3, (branch >> 1) & 3
        return jnp.concatenate(
            [
                gather_a[place_of(partner, partner - (at_z * 4 + at_x), 16), item],
                gather_b[place_of(partner, partner - (at_x * 4 + at_z), 16), item],
            ],
            axis=0,
        )

    field = jnp.zeros((RHS, 128), f32)
    for k in range(4):
        partner = branch_pairs[0, k]
        branch = jnp.maximum(partner, 0)
        pair = jnp.concatenate(halves(branch_coupling_raw[k]), axis=1)
        field = field + apply_nt(gathered(partner, branch, 8 + (branch & 1)), pair)
    pair = jnp.concatenate(halves(transfer_raw[core, s]), axis=1)
    field = apply_nt(split(field), pair)
    for k in range(8):
        partner = node_pairs[s, k]
        at = jnp.maximum(partner, 0)
        branch = at >> 2
        pair = jnp.concatenate(halves(node_coupling_raw[k]), axis=1)
        field = field + apply_nt(gathered(partner, branch, (branch & 1) * 4 + (at & 3)), pair)
    node_field = split(field)
    for q in range(MIDS):
        mid_window[q] = split(mid_field[q] + apply_nt(node_field, mid_transfer_pair[q]))

    out_copies = []
    for part in range(PARTS):

        @pl.loop(0, per // 3)
        def _(step):
            for i in range(3):
                leaf = part * per + step * 3 + i
                field = split(apply_nt(mid_window[leaf_parent[0, leaf]], up_pair[leaf]))
                own = basis_buf[leaf]
                far = nn(field, jnp.concatenate([own, own], axis=0))
                total[:, columns_of(leaf)] += far

        at = pl.ds(part * per * LEAF, per * LEAF)
        copy = pltpu.make_async_copy(total.at[:, at], out.at[:, at], out_sem.at[part])
        copy.start()
        out_copies.append(copy)
    for copy in out_copies:
        copy.wait()
    for copy in sends + to_column + to_mids + to_halo + to_lines + to_planes:
        copy.wait_send()


def on_device(
    right_sides, near_blocks, near_list, leaf_basis, leaf_parent, leaf_upward_matrix, mid_pairs,
    mid_coupling, mid_transfer, node_pairs, node_coupling, node_transfer, branch_pairs,
    branch_coupling,
):
    dma = pltpu.SemaphoreType.DMA
    smem = pl.BlockSpec(memory_space=pltpu.SMEM)
    hbm = pl.BlockSpec(memory_space=pltpu.HBM)
    return pl.pallas_call(
        kernel,
        out_shape=jax.ShapeDtypeStruct((RHS, COLS), f32),
        in_specs=[smem] * 5 + [hbm] * 9,
        out_specs=hbm,
        scratch_shapes=[
            pltpu.VMEM((RHS, COLS), bf16),
            pltpu.VMEM((3 * LEAVES + 1, RHS, LEAF), bf16),
            pltpu.VMEM((LEAVES, NEAR, LEAF, LEAF), bf16),
            pltpu.VMEM((LEAVES, RANK, LEAF), bf16),
            pltpu.VMEM((LEAVES, RANK, RANK), f32),
            pltpu.VMEM((MIDS, 4, RANK, RANK), f32),
            pltpu.VMEM((MIDS, RANK, RANK), f32),
            pltpu.VMEM((8, RANK, RANK), f32),
            pltpu.VMEM((2, 4, RANK, RANK), f32),
            pltpu.VMEM((4, RANK, RANK), f32),
            pltpu.VMEM((LEAVES, RANK, 256), bf16),
            pltpu.VMEM((MIDS, RANK, 256), bf16),
            pltpu.VMEM((LEAVES + 1, RHS, 128), f32),
            pltpu.VMEM((3 * MIDS + 1, RHS, 128), bf16),
            pltpu.VMEM((MIDS, RHS, 128), f32),
            pltpu.VMEM((8, RHS, 128), bf16),
            pltpu.VMEM((17, ITEMS, 16, 128), bf16),
            pltpu.VMEM((17, ITEMS, 16, 128), bf16),
            pltpu.VMEM((RHS, COLS), f32),
            dma((8,)), dma((PARTS,)), dma((2, PARTS)), dma((2, PARTS)), dma((2,)), dma((2,)),
            dma, dma, dma((7,)), dma((7,)), dma((2, 3)), dma((2, 3)), dma((2, 3)), dma((2, 3)),
            dma((PARTS,)),
        ],
        compiler_params=pltpu.CompilerParams(
            collective_id=0, has_side_effects=True, vmem_limit_bytes=62 * 2**20
        ),
        cost_estimate=pl.CostEstimate(
            flops=10**9, bytes_accessed=24 * 10**6, transcendentals=0
        ),
    )(
        near_list.T, leaf_parent, mid_pairs.T, node_pairs, branch_pairs,
        right_sides, near_blocks, leaf_basis, leaf_upward_matrix, mid_coupling, mid_transfer,
        node_coupling, node_transfer, branch_coupling,
    )


def solution(mesh):
    rows = ("branch", "sub")
    return jax.shard_map(
        on_device,
        mesh=mesh,
        in_specs=(
            P(None, rows),
            P(rows, None, None, None),
            P(rows, None),
            P(rows, None, None),
            P(rows, None),
            P(rows, None, None),
            P(rows, None),
            P(rows, None, None, None),
            P(rows, None, None),
            P("branch", None),
            P("branch", None, None, None),
            P("branch", None, None),
            P("branch", None),
            P("branch", None, None, None),
        ),
        out_specs=P(None, rows),
        check_vma=False,
    )
```

```python
import jax
import jax.numpy as jnp
from jax import lax
from jax.experimental import pallas as pl
from jax.experimental.pallas import tpu as pltpu
from jax.sharding import PartitionSpec as P

MESH = pl.DeviceIdType.MESH
f32, bf16 = jnp.float32, jnp.bfloat16
RHS, LEAF, RANK, LEAVES, NEAR, MIDS = 32, 256, 64, 24, 6, 6
COLS = LEAVES * LEAF
PARTS = 4
GROUP = 8
EARLY = 1
SLOTS = 12
ITEMS = 10


def nn(x, w):
    return lax.dot_general(x, w, (((1,), (0,)), ((), ())), preferred_element_type=f32)


def nt(x, w):
    return lax.dot_general(x, w, (((1,), (1,)), ((), ())), preferred_element_type=f32)


def split(value):
    high = value.astype(bf16).astype(f32)
    lane = lax.broadcasted_iota(jnp.int32, value.shape, 1)
    return jnp.where(lane < RANK, high, value - high).astype(bf16)


def halves(w):
    both = jnp.concatenate([w, w], axis=1)
    high = both.astype(bf16)
    return high, (both - high.astype(f32)).astype(bf16)


def pair_of(w):
    return jnp.concatenate(halves(w), axis=1)


def twice(x):
    return jnp.concatenate([x, x], axis=1)


def apply_nn(x, pair):
    high, low = pair[:, :128], pair[:, 128:]
    return nn(twice(x), jnp.concatenate([high, high, low, low], axis=0))


def apply_nt(x, pair):
    return nt(twice(x), jnp.concatenate([pair, pair], axis=0))


def place_of(partner, base, empty):
    absent = -jnp.minimum(partner, 0)
    at = (partner - base) * (1 - absent) + empty * absent
    return jnp.minimum(jnp.maximum(at, 0), empty)


def kernel(
    near_list, leaf_parent, mid_pairs, node_pairs, branch_pairs,
    rhs, blocks, basis, upward, mid_coupling, mid_transfer, node_coupling, node_transfer,
    branch_coupling, out,
    rhs_buf, window, block_buf, basis_buf, up_raw, mid_coupling_raw, mid_transfer_raw,
    node_coupling_raw, transfer_raw, branch_coupling_raw, up_pair, mid_transfer_pair,
    transfer_pair, coupling_pair, raised, mid_window, mid_field, column, line_a, line_b, chosen_a,
    chosen_b, got_a, got_b, total, peer_nodes, peer_branches, choice,
    load_sem, block_sem, halo_send, halo_recv, mid_send, mid_recv, transfer_send, transfer_recv,
    column_send, column_recv, pair_send, pair_recv, line_send, line_recv, plane_send, plane_recv,
    out_sem,
):
    b, s = lax.axis_index("branch"), lax.axis_index("sub")
    core, z, x = b % 2, (b // 2) % 4, b // 8
    me = b * 4 + s
    place = core * 4 + s

    def device(at):
        return (at // 4, at % 4)

    right, left = device((me + 1) % 128), device((me + 127) % 128)
    column_peers = []
    for d in range(1, 8):
        at = (place + d) % 8
        column_peers.append((x * 8 + z * 2 + at // 4, at % 4))
    x_peers = [(((x + d) % 4) * 8 + z * 2 + core, s) for d in (1, 2, 3)]
    z_peers = [(x * 8 + ((z + d) % 4) * 2 + core, s) for d in (1, 2, 3)]
    other_core = (x * 8 + z * 2 + 1 - core, s)
    peers = [right, left] + column_peers + x_peers + z_peers

    barrier = pltpu.get_barrier_semaphore()
    for peer in peers:
        pl.semaphore_signal(barrier, inc=1, device_id=peer, device_id_type=MESH)

    def send(src, dst, send_sem, recv_sem, peer):
        copy = pltpu.make_async_remote_copy(
            src_ref=src, dst_ref=dst, send_sem=send_sem, recv_sem=recv_sem,
            device_id=peer, device_id_type=MESH,
        )
        copy.start()
        return copy

    loads = [
        pltpu.make_async_copy(src, dst, load_sem.at[i])
        for i, (src, dst) in enumerate([
            (rhs, rhs_buf),
            (basis, basis_buf),
            (upward, up_raw),
            (mid_transfer, mid_transfer_raw),
            (node_transfer, transfer_raw.at[core]),
            (mid_coupling, mid_coupling_raw),
            (node_coupling.at[s], node_coupling_raw),
            (branch_coupling.at[0], branch_coupling_raw),
        ])
    ]
    per = LEAVES // PARTS
    block_loads = [
        pltpu.make_async_copy(
            blocks.at[pl.ds(i * per, per)], block_buf.at[pl.ds(i * per, per)], block_sem.at[i]
        )
        for i in range(PARTS)
    ]
    for copy in loads + block_loads:
        copy.start()
    window[3 * LEAVES] = jnp.zeros((RHS, LEAF), bf16)
    mid_window[3 * MIDS] = jnp.zeros((RHS, 128), bf16)
    raised[LEAVES] = jnp.zeros((RHS, 128), f32)
    got_a[4 * SLOTS] = jnp.zeros((16, 128), bf16)
    got_b[4 * SLOTS] = jnp.zeros((16, 128), bf16)

    def columns_of(leaf):
        return pl.ds(pl.multiple_of(leaf * LEAF, LEAF), LEAF)

    for copy in loads[:3]:
        copy.wait()

    for first in range(0, LEAVES, GROUP):
        group = range(first, first + GROUP)
        coefs = []
        for leaf in group:
            values = rhs_buf[:, leaf * LEAF : (leaf + 1) * LEAF]
            window[LEAVES + leaf] = values
            own = basis_buf[leaf]
            coefs.append(nt(values, jnp.concatenate([own, own], axis=0)))
            up_pair[leaf] = pair_of(up_raw[leaf])
        for leaf, coef in zip(group, coefs):
            raised[leaf] = apply_nn(split(coef), up_pair[leaf])

    parents = [leaf_parent[0, leaf] for leaf in range(LEAVES)]
    ends = [0]
    for q in range(1, MIDS):
        below = 0
        for parent in parents:
            below = below + jnp.minimum(jnp.maximum(q - parent, 0), 1)
        ends.append(below)
    ends.append(LEAVES)
    mids = []
    for q in range(MIDS):
        value = raised[ends[q]]
        for i in range(1, 6):
            leaf = ends[q] + i
            past = jnp.minimum(jnp.maximum(leaf + 1 - ends[q + 1], 0), 1)
            value = value + raised[leaf * (1 - past) + LEAVES * past]
        mids.append(value)
    loads[3].wait()
    node = jnp.zeros((RHS, 128), f32)
    for q in range(MIDS):
        pair = jnp.concatenate(halves(mid_transfer_raw[q]), axis=1)
        mid_transfer_pair[q] = pair
        coef = split(mids[q])
        mid_window[MIDS + q] = coef
        node = node + apply_nn(coef, pair)
    column[place] = split(node)

    pl.semaphore_wait(barrier, len(peers))
    to_column = [
        send(column.at[place], column.at[place], column_send.at[d], column_recv.at[d], peer)
        for d, peer in enumerate(column_peers)
    ]
    loads[4].wait()
    to_core = send(
        transfer_raw.at[core], transfer_raw.at[core], transfer_send, transfer_recv, other_core
    )
    to_choose = []
    for d, peer in enumerate(z_peers + x_peers):
        to_choose.append(
            send(node_pairs, peer_nodes.at[d], pair_send.at[0, d], pair_recv.at[0, d], peer)
        )
        to_choose.append(
            send(branch_pairs, peer_branches.at[d], pair_send.at[1, d], pair_recv.at[1, d], peer)
        )

    def halo(i):
        j = PARTS - 1 - i
        return [
            send(window.at[pl.ds(LEAVES + j * per, per)], window.at[pl.ds(j * per, per)],
                 halo_send.at[0, j], halo_recv.at[0, j], right),
            send(window.at[pl.ds(LEAVES + i * per, per)],
                 window.at[pl.ds(2 * LEAVES + i * per, per)],
                 halo_send.at[1, i], halo_recv.at[1, i], left),
        ]

    to_halo = []
    for i in range(EARLY):
        to_halo += halo(i)

    def near_self(part):
        block_loads[part].wait()
        for leaf in range(part * per, part * per + per):
            total[:, leaf * LEAF : (leaf + 1) * LEAF] = nt(
                rhs_buf[:, leaf * LEAF : (leaf + 1) * LEAF], block_buf[leaf, 0]
            )

    for sub in range(4):
        transfer_pair[core * 4 + sub] = pair_of(transfer_raw[core, sub])
    for part in range(PARTS // 2):
        near_self(part)

    to_core.wait_recv()
    for sub in range(4):
        transfer_pair[(1 - core) * 4 + sub] = pair_of(transfer_raw[1 - core, sub])
    for copy in to_column:
        copy.wait_recv()
    for half in range(2):
        top = jnp.zeros((RHS, 128), f32)
        for sub in range(4):
            item = half * 4 + sub
            top = top + apply_nn(column[item], transfer_pair[item])
        top = split(top)
        line_a[x * ITEMS + 8 + half] = top[:16]
        line_b[z * ITEMS + 8 + half] = top[16:]
    for item in range(8):
        value = column[item]
        line_a[x * ITEMS + item] = value[:16]
        line_b[z * ITEMS + item] = value[16:]
    own_a, own_b = line_a.at[pl.ds(x * ITEMS, ITEMS)], line_b.at[pl.ds(z * ITEMS, ITEMS)]
    to_lines = [
        send(own_a, own_a, line_send.at[0, d], line_recv.at[0, d], peer)
        for d, peer in enumerate(x_peers)
    ] + [
        send(own_b, own_b, line_send.at[1, d], line_recv.at[1, d], peer)
        for d, peer in enumerate(z_peers)
    ]
    own_mids = mid_window.at[pl.ds(MIDS, MIDS)]
    to_mids = [
        send(own_mids, mid_window.at[pl.ds(0, MIDS)], mid_send.at[0], mid_recv.at[0], right),
        send(own_mids, mid_window.at[pl.ds(2 * MIDS, MIDS)], mid_send.at[1], mid_recv.at[1], left),
    ]
    for i in range(EARLY, PARTS):
        to_halo += halo(i)

    def spot(node, item):
        branch = node if item else node >> 2
        inside = 8 + (branch & 1) if item else (branch & 1) * 4 + (node & 3)
        return branch >> 3, (branch >> 1) & 3, inside

    for copy in to_choose:
        copy.wait_recv()
    for d in range(6):
        for k in range(SLOTS):
            if k < 4:
                at = spot(jnp.maximum(peer_branches[d, 0, k], 0), True)
            else:
                at = spot(jnp.maximum(peer_nodes[d, s, k - 4], 0), False)
            choice[d * SLOTS + k] = at[0 if d < 3 else 1] * ITEMS + at[2]
    own_choice, absent = [], []
    for k in range(SLOTS):
        partner = branch_pairs[0, k] if k < 4 else node_pairs[s, k - 4]
        own_choice.append(spot(jnp.maximum(partner, 0), k < 4))
        absent.append(partner)

    for part in range(PARTS // 2, PARTS):
        near_self(part)
    for copy in loads[5:]:
        copy.wait()
    for k in range(4):
        coupling_pair[k] = pair_of(branch_coupling_raw[k])
    for k in range(8):
        coupling_pair[4 + k] = pair_of(node_coupling_raw[k])

    for copy in to_lines:
        copy.wait_recv()
    to_planes = []
    for d in range(3):
        for k in range(SLOTS):
            chosen_a[d * SLOTS + k] = line_a[choice[(2 - d) * SLOTS + k]]
            chosen_b[d * SLOTS + k] = line_b[choice[(5 - d) * SLOTS + k]]
        at = pl.ds(d * SLOTS, SLOTS)
        to_planes.append(
            send(chosen_a.at[at], got_a.at[pl.ds(z * SLOTS, SLOTS)],
                 plane_send.at[0, d], plane_recv.at[0, d], z_peers[d])
        )
        to_planes.append(
            send(chosen_b.at[at], got_b.at[pl.ds(x * SLOTS, SLOTS)],
                 plane_send.at[1, d], plane_recv.at[1, d], x_peers[d])
        )
    for k in range(SLOTS):
        at_x, at_z, item = own_choice[k]
        got_a[z * SLOTS + k] = line_a[at_x * ITEMS + item]
        got_b[x * SLOTS + k] = line_b[at_z * ITEMS + item]

    for copy in to_mids:
        copy.wait_recv()
    for q in range(MIDS):
        field = jnp.zeros((RHS, 128), f32)
        for k in range(4):
            at = place_of(mid_pairs[k, q], me * MIDS - MIDS, 3 * MIDS)
            field = field + apply_nt(mid_window[at], pair_of(mid_coupling_raw[q, k]))
        mid_field[q] = field

    for copy in to_halo:
        copy.wait_recv()

    @pl.loop(0, LEAVES // 4)
    def _(step):
        for i in range(4):
            leaf = step * 4 + i
            value = total[:, columns_of(leaf)]
            for k in range(1, NEAR):
                at = place_of(near_list[k, leaf], me * LEAVES - LEAVES, 3 * LEAVES)
                value = value + nt(window[at], block_buf[leaf, k])
            total[:, columns_of(leaf)] = value

    for copy in to_planes:
        copy.wait_recv()

    def gathered(k):
        at_x, at_z, _ = own_choice[k]
        return jnp.concatenate(
            [
                got_a[place_of(absent[k], absent[k] - (at_z * SLOTS + k), 4 * SLOTS)],
                got_b[place_of(absent[k], absent[k] - (at_x * SLOTS + k), 4 * SLOTS)],
            ],
            axis=0,
        )

    field = jnp.zeros((RHS, 128), f32)
    for k in range(4):
        field = field + apply_nt(gathered(k), coupling_pair[k])
    nodes_field = jnp.zeros((RHS, 128), f32)
    for k in range(4, SLOTS):
        nodes_field = nodes_field + apply_nt(gathered(k), coupling_pair[k])
    field = nodes_field + apply_nt(split(field), transfer_pair[place])
    node_field = split(field)
    for q in range(MIDS):
        mid_window[q] = split(mid_field[q] + apply_nt(node_field, mid_transfer_pair[q]))

    out_copies = []
    for part in range(PARTS):
        group = range(part * per, part * per + per)
        fields = [split(apply_nt(mid_window[leaf_parent[0, leaf]], up_pair[leaf])) for leaf in group]
        for leaf, field in zip(group, fields):
            own = basis_buf[leaf]
            far = nn(field, jnp.concatenate([own, own], axis=0))
            total[:, leaf * LEAF : (leaf + 1) * LEAF] += far
        at = pl.ds(part * per * LEAF, per * LEAF)
        copy = pltpu.make_async_copy(total.at[:, at], out.at[:, at], out_sem.at[part])
        copy.start()
        out_copies.append(copy)
    for copy in out_copies:
        copy.wait()
    for copy in [to_core] + to_column + to_choose + to_mids + to_halo + to_lines + to_planes:
        copy.wait_send()


def on_device(
    right_sides, near_blocks, near_list, leaf_basis, leaf_parent, leaf_upward_matrix, mid_pairs,
    mid_coupling, mid_transfer, node_pairs, node_coupling, node_transfer, branch_pairs,
    branch_coupling,
):
    dma = pltpu.SemaphoreType.DMA
    smem = pl.BlockSpec(memory_space=pltpu.SMEM)
    hbm = pl.BlockSpec(memory_space=pltpu.HBM)
    return pl.pallas_call(
        kernel,
        out_shape=jax.ShapeDtypeStruct((RHS, COLS), f32),
        in_specs=[smem] * 5 + [hbm] * 9,
        out_specs=hbm,
        scratch_shapes=[
            pltpu.VMEM((RHS, COLS), bf16),
            pltpu.VMEM((3 * LEAVES + 1, RHS, LEAF), bf16),
            pltpu.VMEM((LEAVES, NEAR, LEAF, LEAF), bf16),
            pltpu.VMEM((LEAVES, RANK, LEAF), bf16),
            pltpu.VMEM((LEAVES, RANK, RANK), f32),
            pltpu.VMEM((MIDS, 4, RANK, RANK), f32),
            pltpu.VMEM((MIDS, RANK, RANK), f32),
            pltpu.VMEM((8, RANK, RANK), f32),
            pltpu.VMEM((2, 4, RANK, RANK), f32),
            pltpu.VMEM((4, RANK, RANK), f32),
            pltpu.VMEM((LEAVES, RANK, 256), bf16),
            pltpu.VMEM((MIDS, RANK, 256), bf16),
            pltpu.VMEM((8, RANK, 256), bf16),
            pltpu.VMEM((SLOTS, RANK, 256), bf16),
            pltpu.VMEM((LEAVES + 1, RHS, 128), f32),
            pltpu.VMEM((3 * MIDS + 1, RHS, 128), bf16),
            pltpu.VMEM((MIDS, RHS, 128), f32),
            pltpu.VMEM((8, RHS, 128), bf16),
            pltpu.VMEM((4 * ITEMS, 16, 128), bf16),
            pltpu.VMEM((4 * ITEMS, 16, 128), bf16),
            pltpu.VMEM((3 * SLOTS, 16, 128), bf16),
            pltpu.VMEM((3 * SLOTS, 16, 128), bf16),
            pltpu.VMEM((4 * SLOTS + 1, 16, 128), bf16),
            pltpu.VMEM((4 * SLOTS + 1, 16, 128), bf16),
            pltpu.VMEM((RHS, COLS), f32),
            pltpu.SMEM((6, 4, 8), jnp.int32),
            pltpu.SMEM((6, 1, 4), jnp.int32),
            pltpu.SMEM((6 * SLOTS,), jnp.int32),
            dma((8,)), dma((PARTS,)), dma((2, PARTS)), dma((2, PARTS)), dma((2,)), dma((2,)),
            dma, dma, dma((7,)), dma((7,)), dma((2, 6)), dma((2, 6)), dma((2, 3)), dma((2, 3)), dma((2, 3)), dma((2, 3)),
            dma((PARTS,)),
        ],
        compiler_params=pltpu.CompilerParams(
            collective_id=0, has_side_effects=True, vmem_limit_bytes=62 * 2**20
        ),
        cost_estimate=pl.CostEstimate(
            flops=10**9, bytes_accessed=24 * 10**6, transcendentals=0
        ),
    )(
        near_list.T, leaf_parent, mid_pairs.T, node_pairs, branch_pairs,
        right_sides, near_blocks, leaf_basis, leaf_upward_matrix, mid_coupling, mid_transfer,
        node_coupling, node_transfer, branch_coupling,
    )


def solution(mesh):
    rows = ("branch", "sub")
    return jax.shard_map(
        on_device,
        mesh=mesh,
        in_specs=(
            P(None, rows),
            P(rows, None, None, None),
            P(rows, None),
            P(rows, None, None),
            P(rows, None),
            P(rows, None, None),
            P(rows, None),
            P(rows, None, None, None),
            P(rows, None, None),
            P("branch", None),
            P("branch", None, None, None),
            P("branch", None, None),
            P("branch", None),
            P("branch", None, None, None),
        ),
        out_specs=P(None, rows),
        check_vma=False,
    )
```

```python
import jax
import jax.numpy as jnp
from jax import lax
from jax.experimental import pallas as pl
from jax.experimental.pallas import tpu as pltpu
from jax.sharding import PartitionSpec as P

MESH = pl.DeviceIdType.MESH
f32, bf16 = jnp.float32, jnp.bfloat16
RHS, LEAF, RANK, LEAVES, NEAR, MIDS = 32, 256, 64, 24, 6, 6
COLS = LEAVES * LEAF
PARTS = 4
GROUP = 8
THIRD = 3
STAGES = 4
FIRST = LEAVES - (STAGES - 1) * THIRD
SECOND = 12
BESIDE_LINE = 1
SLOTS = 12
ITEMS = 10


def nn(x, w):
    return lax.dot_general(x, w, (((1,), (0,)), ((), ())), preferred_element_type=f32)


def nt(x, w):
    return lax.dot_general(x, w, (((1,), (1,)), ((), ())), preferred_element_type=f32)


def split(value):
    high = value.astype(bf16).astype(f32)
    lane = lax.broadcasted_iota(jnp.int32, value.shape, 1)
    return jnp.where(lane < RANK, high, value - high).astype(bf16)


def halves(w):
    both = jnp.concatenate([w, w], axis=1)
    high = both.astype(bf16)
    return high, (both - high.astype(f32)).astype(bf16)


def pair_of(w):
    return jnp.concatenate(halves(w), axis=1)


def twice(x):
    return jnp.concatenate([x, x], axis=1)


def apply_nn(x, pair):
    high, low = pair[:, :128], pair[:, 128:]
    return nn(twice(x), jnp.concatenate([high, high, low, low], axis=0))


def apply_nt(x, pair):
    return nt(twice(x), jnp.concatenate([pair, pair], axis=0))


def place_of(partner, base, empty):
    absent = -jnp.minimum(partner, 0)
    at = (partner - base) * (1 - absent) + empty * absent
    return jnp.minimum(jnp.maximum(at, 0), empty)


def kernel(
    near_list, leaf_parent, mid_pairs, node_pairs, branch_pairs,
    rhs, blocks, basis, upward, mid_coupling, mid_transfer, node_coupling, node_transfer,
    branch_coupling, out,
    rhs_buf, window, late, block_buf, basis_buf, up_raw, mid_coupling_raw, mid_transfer_raw,
    node_coupling_raw, transfer_raw, branch_coupling_raw, up_pair, mid_transfer_pair,
    transfer_pair, coupling_pair, raised, mid_window, mid_field, column, line_a, line_b, chosen_a,
    chosen_b, got_a, got_b, total, peer_nodes, peer_branches, choice,
    load_sem, block_sem, halo_send, halo_recv, mid_send, mid_recv, transfer_send, transfer_recv,
    column_send, column_recv, pair_send, pair_recv, line_send, line_recv, plane_send, plane_recv,
    out_sem,
):
    b, s = lax.axis_index("branch"), lax.axis_index("sub")
    core, z, x = b % 2, (b // 2) % 4, b // 8
    me = b * 4 + s
    place = core * 4 + s

    def device(at):
        return (at // 4, at % 4)

    right, left = device((me + 1) % 128), device((me + 127) % 128)
    column_peers = []
    for d in range(1, 8):
        at = (place + d) % 8
        column_peers.append((x * 8 + z * 2 + at // 4, at % 4))
    x_peers = [(((x + d) % 4) * 8 + z * 2 + core, s) for d in (1, 2, 3)]
    z_peers = [(x * 8 + ((z + d) % 4) * 2 + core, s) for d in (1, 2, 3)]
    other_core = (x * 8 + z * 2 + 1 - core, s)
    peers = [right, left] + column_peers + x_peers + z_peers

    barrier = pltpu.get_barrier_semaphore()
    for peer in peers:
        pl.semaphore_signal(barrier, inc=1, device_id=peer, device_id_type=MESH)

    def send(src, dst, send_sem, recv_sem, peer):
        copy = pltpu.make_async_remote_copy(
            src_ref=src, dst_ref=dst, send_sem=send_sem, recv_sem=recv_sem,
            device_id=peer, device_id_type=MESH,
        )
        copy.start()
        return copy

    loads = [
        pltpu.make_async_copy(src, dst, load_sem.at[i])
        for i, (src, dst) in enumerate([
            (rhs, rhs_buf),
            (basis, basis_buf),
            (upward, up_raw),
            (mid_transfer, mid_transfer_raw),
            (node_transfer, transfer_raw.at[core]),
            (mid_coupling, mid_coupling_raw),
            (node_coupling.at[s], node_coupling_raw),
            (branch_coupling.at[0], branch_coupling_raw),
        ])
    ]
    per = LEAVES // PARTS
    block_loads = [
        pltpu.make_async_copy(
            blocks.at[pl.ds(i * per, per)], block_buf.at[pl.ds(i * per, per)], block_sem.at[i]
        )
        for i in range(PARTS)
    ]
    for copy in loads[:3]:
        copy.start()
    for leaf in [*range(LEAVES - FIRST), *range(2 * LEAVES + FIRST, 3 * LEAVES + 1)]:
        window[leaf] = jnp.zeros((RHS, LEAF), bf16)
    mid_window[3 * MIDS] = jnp.zeros((RHS, 128), bf16)
    raised[LEAVES] = jnp.zeros((RHS, 128), f32)
    got_a[4 * SLOTS] = jnp.zeros((16, 128), bf16)
    got_b[4 * SLOTS] = jnp.zeros((16, 128), bf16)

    def columns_of(leaf):
        return pl.ds(pl.multiple_of(leaf * LEAF, LEAF), LEAF)

    for copy in loads[:3]:
        copy.wait()
    for copy in loads[3:] + block_loads:
        copy.start()
    for leaf in range(LEAVES):
        window[LEAVES + leaf] = rhs_buf[:, leaf * LEAF : (leaf + 1) * LEAF]
    def send_halo(stage):
        if stage < 0:
            size = -stage
            begin = FIRST - size if stage == -SECOND else 0
            end = begin + size
            there = [window.at[pl.ds(LEAVES - end, size)], window.at[pl.ds(2 * LEAVES + begin, size)]]
        else:
            size, end = THIRD, FIRST + (stage + 1) * THIRD
            there = [late.at[stage, 0], late.at[stage, 1]]
        here = [window.at[pl.ds(2 * LEAVES - end, size)], window.at[pl.ds(LEAVES + end - size, size)]]
        slot = stage + 2 if stage >= 0 else (1 if stage == -SECOND else 0)
        return [
            send(here[i], there[i], halo_send.at[i, slot], halo_recv.at[i, slot], peer)
            for i, peer in enumerate((right, left))
        ]


    for first in range(0, LEAVES, GROUP):
        group = range(first, first + GROUP)
        coefs = []
        for leaf in group:
            values = rhs_buf[:, leaf * LEAF : (leaf + 1) * LEAF]
            own = basis_buf[leaf]
            coefs.append(nt(values, jnp.concatenate([own, own], axis=0)))
            up_pair[leaf] = pair_of(up_raw[leaf])
        for leaf, coef in zip(group, coefs):
            raised[leaf] = apply_nn(split(coef), up_pair[leaf])

    pl.semaphore_wait(barrier, len(peers))
    to_halo = send_halo(SECOND - FIRST)

    parents = [leaf_parent[0, leaf] for leaf in range(LEAVES)]
    ends = [0]
    for q in range(1, MIDS):
        below = 0
        for parent in parents:
            below = below + jnp.minimum(jnp.maximum(q - parent, 0), 1)
        ends.append(below)
    ends.append(LEAVES)
    mids = []
    for q in range(MIDS):
        value = raised[ends[q]]
        for i in range(1, 6):
            leaf = ends[q] + i
            past = jnp.minimum(jnp.maximum(leaf + 1 - ends[q + 1], 0), 1)
            value = value + raised[leaf * (1 - past) + LEAVES * past]
        mids.append(value)
    loads[3].wait()
    node = jnp.zeros((RHS, 128), f32)
    for q in range(MIDS):
        pair = jnp.concatenate(halves(mid_transfer_raw[q]), axis=1)
        mid_transfer_pair[q] = pair
        coef = split(mids[q])
        mid_window[MIDS + q] = coef
        node = node + apply_nn(coef, pair)
    column[place] = split(node)

    to_column = [
        send(column.at[place], column.at[place], column_send.at[d], column_recv.at[d], peer)
        for d, peer in enumerate(column_peers)
    ]
    loads[4].wait()
    to_core = send(
        transfer_raw.at[core], transfer_raw.at[core], transfer_send, transfer_recv, other_core
    )
    to_choose = []
    for d, peer in enumerate(z_peers + x_peers):
        to_choose.append(
            send(node_pairs, peer_nodes.at[d], pair_send.at[0, d], pair_recv.at[0, d], peer)
        )
        to_choose.append(
            send(branch_pairs, peer_branches.at[d], pair_send.at[1, d], pair_recv.at[1, d], peer)
        )

    own_mids = mid_window.at[pl.ds(MIDS, MIDS)]
    to_mids = [
        send(own_mids, mid_window.at[pl.ds(0, MIDS)], mid_send.at[0], mid_recv.at[0], right),
        send(own_mids, mid_window.at[pl.ds(2 * MIDS, MIDS)], mid_send.at[1], mid_recv.at[1], left),
    ]
    to_halo += send_halo(-SECOND)
    for stage in range(STAGES - 1):
        to_halo += send_halo(stage)

    def near_self(part):
        block_loads[part].wait()
        for leaf in range(part * per, part * per + per):
            total[:, leaf * LEAF : (leaf + 1) * LEAF] = nt(
                rhs_buf[:, leaf * LEAF : (leaf + 1) * LEAF], block_buf[leaf, 0]
            )

    for sub in range(4):
        transfer_pair[core * 4 + sub] = pair_of(transfer_raw[core, sub])
    for part in range(PARTS // 2):
        near_self(part)

    to_core.wait_recv()
    for sub in range(4):
        transfer_pair[(1 - core) * 4 + sub] = pair_of(transfer_raw[1 - core, sub])
    for copy in to_column:
        copy.wait_recv()
    for half in range(2):
        top = jnp.zeros((RHS, 128), f32)
        for sub in range(4):
            item = half * 4 + sub
            top = top + apply_nn(column[item], transfer_pair[item])
        top = split(top)
        line_a[x * ITEMS + 8 + half] = top[:16]
        line_b[z * ITEMS + 8 + half] = top[16:]
    for item in range(8):
        value = column[item]
        line_a[x * ITEMS + item] = value[:16]
        line_b[z * ITEMS + item] = value[16:]
    own_a, own_b = line_a.at[pl.ds(x * ITEMS, ITEMS)], line_b.at[pl.ds(z * ITEMS, ITEMS)]
    to_lines = [
        send(own_a, own_a, line_send.at[0, d], line_recv.at[0, d], peer)
        for d, peer in enumerate(x_peers)
    ] + [
        send(own_b, own_b, line_send.at[1, d], line_recv.at[1, d], peer)
        for d, peer in enumerate(z_peers)
    ]

    def near_others(stage):
        for copy in to_halo[2 * stage + 2 : 2 * stage + 4] if stage else to_halo[:4]:
            copy.wait_recv()
        end = FIRST + stage * THIRD
        if stage:
            for i in range(THIRD):
                window[LEAVES - end + i] = late[stage - 1, 0, i]
                window[2 * LEAVES + end - THIRD + i] = late[stage - 1, 1, i]
            leaves = [*range(LEAVES - end, LEAVES - end + THIRD), *range(end - THIRD, end)]
        else:
            leaves = range(LEAVES - end, end)
        for leaf in leaves:
            value = total[:, leaf * LEAF : (leaf + 1) * LEAF]
            for k in range(1, NEAR):
                at = place_of(near_list[k, leaf], me * LEAVES - LEAVES, 3 * LEAVES)
                value = value + nt(window[at], block_buf[leaf, k])
            total[:, leaf * LEAF : (leaf + 1) * LEAF] = value

    def spot(node, item):
        branch = node if item else node >> 2
        inside = 8 + (branch & 1) if item else (branch & 1) * 4 + (node & 3)
        return branch >> 3, (branch >> 1) & 3, inside

    for copy in to_choose:
        copy.wait_recv()
    for d in range(6):
        for k in range(SLOTS):
            if k < 4:
                at = spot(jnp.maximum(peer_branches[d, 0, k], 0), True)
            else:
                at = spot(jnp.maximum(peer_nodes[d, s, k - 4], 0), False)
            choice[d * SLOTS + k] = at[0 if d < 3 else 1] * ITEMS + at[2]
    own_choice, absent = [], []
    for k in range(SLOTS):
        partner = branch_pairs[0, k] if k < 4 else node_pairs[s, k - 4]
        own_choice.append(spot(jnp.maximum(partner, 0), k < 4))
        absent.append(partner)

    for part in range(PARTS // 2, PARTS):
        near_self(part)
    for copy in loads[5:]:
        copy.wait()
    for k in range(4):
        coupling_pair[k] = pair_of(branch_coupling_raw[k])
    for k in range(8):
        coupling_pair[4 + k] = pair_of(node_coupling_raw[k])

    for stage in range(BESIDE_LINE):
        near_others(stage)

    for copy in to_lines:
        copy.wait_recv()
    to_planes = []
    for d in range(3):
        for k in range(SLOTS):
            chosen_a[d * SLOTS + k] = line_a[choice[(2 - d) * SLOTS + k]]
            chosen_b[d * SLOTS + k] = line_b[choice[(5 - d) * SLOTS + k]]
        at = pl.ds(d * SLOTS, SLOTS)
        to_planes.append(
            send(chosen_a.at[at], got_a.at[pl.ds(z * SLOTS, SLOTS)],
                 plane_send.at[0, d], plane_recv.at[0, d], z_peers[d])
        )
        to_planes.append(
            send(chosen_b.at[at], got_b.at[pl.ds(x * SLOTS, SLOTS)],
                 plane_send.at[1, d], plane_recv.at[1, d], x_peers[d])
        )
    for k in range(SLOTS):
        at_x, at_z, item = own_choice[k]
        got_a[z * SLOTS + k] = line_a[at_x * ITEMS + item]
        got_b[x * SLOTS + k] = line_b[at_z * ITEMS + item]

    for copy in to_mids:
        copy.wait_recv()
    for q in range(MIDS):
        field = jnp.zeros((RHS, 128), f32)
        for k in range(4):
            at = place_of(mid_pairs[k, q], me * MIDS - MIDS, 3 * MIDS)
            field = field + apply_nt(mid_window[at], pair_of(mid_coupling_raw[q, k]))
        mid_field[q] = field

    for stage in range(BESIDE_LINE, STAGES):
        near_others(stage)

    for copy in to_planes:
        copy.wait_recv()

    def gathered(k):
        at_x, at_z, _ = own_choice[k]
        return jnp.concatenate(
            [
                got_a[place_of(absent[k], absent[k] - (at_z * SLOTS + k), 4 * SLOTS)],
                got_b[place_of(absent[k], absent[k] - (at_x * SLOTS + k), 4 * SLOTS)],
            ],
            axis=0,
        )

    field = jnp.zeros((RHS, 128), f32)
    for k in range(4):
        field = field + apply_nt(gathered(k), coupling_pair[k])
    nodes_field = jnp.zeros((RHS, 128), f32)
    for k in range(4, SLOTS):
        nodes_field = nodes_field + apply_nt(gathered(k), coupling_pair[k])
    field = nodes_field + apply_nt(split(field), transfer_pair[place])
    node_field = split(field)
    for q in range(MIDS):
        mid_window[q] = split(mid_field[q] + apply_nt(node_field, mid_transfer_pair[q]))

    out_copies = []
    for part in range(PARTS):
        group = range(part * per, part * per + per)
        fields = [split(apply_nt(mid_window[leaf_parent[0, leaf]], up_pair[leaf])) for leaf in group]
        for leaf, field in zip(group, fields):
            own = basis_buf[leaf]
            far = nn(field, jnp.concatenate([own, own], axis=0))
            total[:, leaf * LEAF : (leaf + 1) * LEAF] += far
        at = pl.ds(part * per * LEAF, per * LEAF)
        copy = pltpu.make_async_copy(total.at[:, at], out.at[:, at], out_sem.at[part])
        copy.start()
        out_copies.append(copy)
    for copy in out_copies:
        copy.wait()
    for copy in [to_core] + to_column + to_choose + to_mids + to_halo + to_lines + to_planes:
        copy.wait_send()


def on_device(
    right_sides, near_blocks, near_list, leaf_basis, leaf_parent, leaf_upward_matrix, mid_pairs,
    mid_coupling, mid_transfer, node_pairs, node_coupling, node_transfer, branch_pairs,
    branch_coupling,
):
    dma = pltpu.SemaphoreType.DMA
    smem = pl.BlockSpec(memory_space=pltpu.SMEM)
    hbm = pl.BlockSpec(memory_space=pltpu.HBM)
    return pl.pallas_call(
        kernel,
        out_shape=jax.ShapeDtypeStruct((RHS, COLS), f32),
        in_specs=[smem] * 5 + [hbm] * 9,
        out_specs=hbm,
        scratch_shapes=[
            pltpu.VMEM((RHS, COLS), bf16),
            pltpu.VMEM((3 * LEAVES + 1, RHS, LEAF), bf16),
            pltpu.VMEM((STAGES - 1, 2, THIRD, RHS, LEAF), bf16),
            pltpu.VMEM((LEAVES, NEAR, LEAF, LEAF), bf16),
            pltpu.VMEM((LEAVES, RANK, LEAF), bf16),
            pltpu.VMEM((LEAVES, RANK, RANK), f32),
            pltpu.VMEM((MIDS, 4, RANK, RANK), f32),
            pltpu.VMEM((MIDS, RANK, RANK), f32),
            pltpu.VMEM((8, RANK, RANK), f32),
            pltpu.VMEM((2, 4, RANK, RANK), f32),
            pltpu.VMEM((4, RANK, RANK), f32),
            pltpu.VMEM((LEAVES, RANK, 256), bf16),
            pltpu.VMEM((MIDS, RANK, 256), bf16),
            pltpu.VMEM((8, RANK, 256), bf16),
            pltpu.VMEM((SLOTS, RANK, 256), bf16),
            pltpu.VMEM((LEAVES + 1, RHS, 128), f32),
            pltpu.VMEM((3 * MIDS + 1, RHS, 128), bf16),
            pltpu.VMEM((MIDS, RHS, 128), f32),
            pltpu.VMEM((8, RHS, 128), bf16),
            pltpu.VMEM((4 * ITEMS, 16, 128), bf16),
            pltpu.VMEM((4 * ITEMS, 16, 128), bf16),
            pltpu.VMEM((3 * SLOTS, 16, 128), bf16),
            pltpu.VMEM((3 * SLOTS, 16, 128), bf16),
            pltpu.VMEM((4 * SLOTS + 1, 16, 128), bf16),
            pltpu.VMEM((4 * SLOTS + 1, 16, 128), bf16),
            pltpu.VMEM((RHS, COLS), f32),
            pltpu.SMEM((6, 4, 8), jnp.int32),
            pltpu.SMEM((6, 1, 4), jnp.int32),
            pltpu.SMEM((6 * SLOTS,), jnp.int32),
            dma((8,)), dma((PARTS,)), dma((2, STAGES + 1)), dma((2, STAGES + 1)), dma((2,)), dma((2,)),
            dma, dma, dma((7,)), dma((7,)), dma((2, 6)), dma((2, 6)), dma((2, 3)), dma((2, 3)), dma((2, 3)), dma((2, 3)),
            dma((PARTS,)),
        ],
        compiler_params=pltpu.CompilerParams(
            collective_id=0, has_side_effects=True, vmem_limit_bytes=62 * 2**20
        ),
        cost_estimate=pl.CostEstimate(
            flops=10**9, bytes_accessed=24 * 10**6, transcendentals=0
        ),
    )(
        near_list.T, leaf_parent, mid_pairs.T, node_pairs, branch_pairs,
        right_sides, near_blocks, leaf_basis, leaf_upward_matrix, mid_coupling, mid_transfer,
        node_coupling, node_transfer, branch_coupling,
    )


def solution(mesh):
    rows = ("branch", "sub")
    return jax.shard_map(
        on_device,
        mesh=mesh,
        in_specs=(
            P(None, rows),
            P(rows, None, None, None),
            P(rows, None),
            P(rows, None, None),
            P(rows, None),
            P(rows, None, None),
            P(rows, None),
            P(rows, None, None, None),
            P(rows, None, None),
            P("branch", None),
            P("branch", None, None, None),
            P("branch", None, None),
            P("branch", None),
            P("branch", None, None, None),
        ),
        out_specs=P(None, rows),
        check_vma=False,
    )
```

```python
import jax
import jax.numpy as jnp
from jax import lax
from jax.experimental import pallas as pl
from jax.experimental.pallas import tpu as pltpu
from jax.sharding import PartitionSpec as P

MESH = pl.DeviceIdType.MESH
f32, bf16 = jnp.float32, jnp.bfloat16
RHS, LEAF, RANK, LEAVES, NEAR, MIDS = 32, 256, 64, 24, 6, 6
COLS = LEAVES * LEAF
PARTS = 4
GROUP = 8
THIRD = 3
STAGES = 4
FIRST = LEAVES - (STAGES - 1) * THIRD
SECOND = 12
BESIDE_LINE = 1
SLOTS = 12
ITEMS = 10


def nn(x, w):
    return lax.dot_general(x, w, (((1,), (0,)), ((), ())), preferred_element_type=f32)


def nt(x, w):
    return lax.dot_general(x, w, (((1,), (1,)), ((), ())), preferred_element_type=f32)


def split(value):
    high = value.astype(bf16).astype(f32)
    lane = lax.broadcasted_iota(jnp.int32, value.shape, 1)
    return jnp.where(lane < RANK, high, value - high).astype(bf16)


def halves(w):
    both = jnp.concatenate([w, w], axis=1)
    high = both.astype(bf16)
    return high, (both - high.astype(f32)).astype(bf16)


def pair_of(w):
    return jnp.concatenate(halves(w), axis=1)


def twice(x):
    return jnp.concatenate([x, x], axis=1)


def apply_nn(x, pair):
    high, low = pair[:, :128], pair[:, 128:]
    return nn(twice(x), jnp.concatenate([high, high, low, low], axis=0))


def apply_nt(x, pair):
    return nt(twice(x), jnp.concatenate([pair, pair], axis=0))


def place_of(partner, base, empty):
    absent = -jnp.minimum(partner, 0)
    at = (partner - base) * (1 - absent) + empty * absent
    return jnp.minimum(jnp.maximum(at, 0), empty)


def kernel(
    near_list, leaf_parent, mid_pairs, node_pairs, branch_pairs,
    rhs, blocks, basis, upward, mid_coupling, mid_transfer, node_coupling, node_transfer,
    branch_coupling, total,
    rhs_buf, window, late, block_buf, basis_buf, up_raw, mid_coupling_raw, mid_transfer_raw,
    node_coupling_raw, transfer_raw, branch_coupling_raw, up_pair, mid_transfer_pair,
    transfer_pair, coupling_pair, raised, mid_window, mid_field, column, line_a, line_b, chosen_a,
    chosen_b, got_a, got_b, peer_nodes, peer_branches, choice,
    load_sem, block_sem, halo_send, halo_recv, mid_send, mid_recv, transfer_send, transfer_recv,
    column_send, column_recv, pair_send, pair_recv, line_send, line_recv, plane_send, plane_recv,
):
    b, s = lax.axis_index("branch"), lax.axis_index("sub")
    core, z, x = b % 2, (b // 2) % 4, b // 8
    me = b * 4 + s
    place = core * 4 + s

    def device(at):
        return (at // 4, at % 4)

    right, left = device((me + 1) % 128), device((me + 127) % 128)
    column_peers = []
    for d in range(1, 8):
        at = (place + d) % 8
        column_peers.append((x * 8 + z * 2 + at // 4, at % 4))
    x_peers = [(((x + d) % 4) * 8 + z * 2 + core, s) for d in (1, 2, 3)]
    z_peers = [(x * 8 + ((z + d) % 4) * 2 + core, s) for d in (1, 2, 3)]
    other_core = (x * 8 + z * 2 + 1 - core, s)
    peers = [right, left] + column_peers + x_peers + z_peers

    barrier = pltpu.get_barrier_semaphore()
    for peer in peers:
        pl.semaphore_signal(barrier, inc=1, device_id=peer, device_id_type=MESH)

    def send(src, dst, send_sem, recv_sem, peer):
        copy = pltpu.make_async_remote_copy(
            src_ref=src, dst_ref=dst, send_sem=send_sem, recv_sem=recv_sem,
            device_id=peer, device_id_type=MESH,
        )
        copy.start()
        return copy

    loads = [
        pltpu.make_async_copy(src, dst, load_sem.at[i])
        for i, (src, dst) in enumerate([
            (rhs, rhs_buf),
            (basis, basis_buf),
            (upward, up_raw),
            (mid_transfer, mid_transfer_raw),
            (node_transfer, transfer_raw.at[core]),
            (mid_coupling, mid_coupling_raw),
            (node_coupling.at[s], node_coupling_raw),
            (branch_coupling.at[0], branch_coupling_raw),
        ])
    ]
    per = LEAVES // PARTS
    block_loads = [
        pltpu.make_async_copy(
            blocks.at[pl.ds(i * per, per)], block_buf.at[pl.ds(i * per, per)], block_sem.at[i]
        )
        for i in range(PARTS)
    ]
    for copy in loads[:3]:
        copy.start()
    for leaf in [*range(LEAVES - FIRST), *range(2 * LEAVES + FIRST, 3 * LEAVES + 1)]:
        window[leaf] = jnp.zeros((RHS, LEAF), bf16)
    mid_window[3 * MIDS] = jnp.zeros((RHS, 128), bf16)
    raised[LEAVES] = jnp.zeros((RHS, 128), f32)
    got_a[4 * SLOTS] = jnp.zeros((16, 128), bf16)
    got_b[4 * SLOTS] = jnp.zeros((16, 128), bf16)

    def columns_of(leaf):
        return pl.ds(pl.multiple_of(leaf * LEAF, LEAF), LEAF)

    for copy in loads[:3]:
        copy.wait()
    for copy in loads[3:] + block_loads:
        copy.start()
    for leaf in range(LEAVES):
        window[LEAVES + leaf] = rhs_buf[:, leaf * LEAF : (leaf + 1) * LEAF]
    def send_halo(stage):
        if stage < 0:
            size = -stage
            begin = FIRST - size if stage == -SECOND else 0
            end = begin + size
            there = [window.at[pl.ds(LEAVES - end, size)], window.at[pl.ds(2 * LEAVES + begin, size)]]
        else:
            size, end = THIRD, FIRST + (stage + 1) * THIRD
            there = [late.at[stage, 0], late.at[stage, 1]]
        here = [window.at[pl.ds(2 * LEAVES - end, size)], window.at[pl.ds(LEAVES + end - size, size)]]
        slot = stage + 2 if stage >= 0 else (1 if stage == -SECOND else 0)
        return [
            send(here[i], there[i], halo_send.at[i, slot], halo_recv.at[i, slot], peer)
            for i, peer in enumerate((right, left))
        ]


    for first in range(0, LEAVES, GROUP):
        group = range(first, first + GROUP)
        coefs = []
        for leaf in group:
            values = rhs_buf[:, leaf * LEAF : (leaf + 1) * LEAF]
            own = basis_buf[leaf]
            coefs.append(nt(values, jnp.concatenate([own, own], axis=0)))
            up_pair[leaf] = pair_of(up_raw[leaf])
        for leaf, coef in zip(group, coefs):
            raised[leaf] = apply_nn(split(coef), up_pair[leaf])

    pl.semaphore_wait(barrier, len(peers))
    to_halo = send_halo(SECOND - FIRST)

    parents = [leaf_parent[0, leaf] for leaf in range(LEAVES)]
    ends = [0]
    for q in range(1, MIDS):
        below = 0
        for parent in parents:
            below = below + jnp.minimum(jnp.maximum(q - parent, 0), 1)
        ends.append(below)
    ends.append(LEAVES)
    mids = []
    for q in range(MIDS):
        value = raised[ends[q]]
        for i in range(1, 6):
            leaf = ends[q] + i
            past = jnp.minimum(jnp.maximum(leaf + 1 - ends[q + 1], 0), 1)
            value = value + raised[leaf * (1 - past) + LEAVES * past]
        mids.append(value)
    loads[3].wait()
    node = jnp.zeros((RHS, 128), f32)
    for q in range(MIDS):
        pair = jnp.concatenate(halves(mid_transfer_raw[q]), axis=1)
        mid_transfer_pair[q] = pair
        coef = split(mids[q])
        mid_window[MIDS + q] = coef
        node = node + apply_nn(coef, pair)
    column[place] = split(node)

    to_column = [
        send(column.at[place], column.at[place], column_send.at[d], column_recv.at[d], peer)
        for d, peer in enumerate(column_peers)
    ]
    loads[4].wait()
    to_core = send(
        transfer_raw.at[core], transfer_raw.at[core], transfer_send, transfer_recv, other_core
    )
    to_choose = []
    for d, peer in enumerate(z_peers + x_peers):
        to_choose.append(
            send(node_pairs, peer_nodes.at[d], pair_send.at[0, d], pair_recv.at[0, d], peer)
        )
        to_choose.append(
            send(branch_pairs, peer_branches.at[d], pair_send.at[1, d], pair_recv.at[1, d], peer)
        )

    own_mids = mid_window.at[pl.ds(MIDS, MIDS)]
    to_mids = [
        send(own_mids, mid_window.at[pl.ds(0, MIDS)], mid_send.at[0], mid_recv.at[0], right),
        send(own_mids, mid_window.at[pl.ds(2 * MIDS, MIDS)], mid_send.at[1], mid_recv.at[1], left),
    ]
    to_halo += send_halo(-SECOND)

    def near_self(part):
        block_loads[part].wait()
        for leaf in range(part * per, part * per + per):
            total[:, leaf * LEAF : (leaf + 1) * LEAF] = nt(
                rhs_buf[:, leaf * LEAF : (leaf + 1) * LEAF], block_buf[leaf, 0]
            )

    for sub in range(4):
        transfer_pair[core * 4 + sub] = pair_of(transfer_raw[core, sub])
    for part in range(PARTS // 2):
        near_self(part)

    to_core.wait_recv()
    for sub in range(4):
        transfer_pair[(1 - core) * 4 + sub] = pair_of(transfer_raw[1 - core, sub])
    for copy in to_column:
        copy.wait_recv()
    for stage in range(STAGES - 1):
        to_halo += send_halo(stage)
    for half in range(2):
        top = jnp.zeros((RHS, 128), f32)
        for sub in range(4):
            item = half * 4 + sub
            top = top + apply_nn(column[item], transfer_pair[item])
        top = split(top)
        line_a[x * ITEMS + 8 + half] = top[:16]
        line_b[z * ITEMS + 8 + half] = top[16:]
    for item in range(8):
        value = column[item]
        line_a[x * ITEMS + item] = value[:16]
        line_b[z * ITEMS + item] = value[16:]
    own_a, own_b = line_a.at[pl.ds(x * ITEMS, ITEMS)], line_b.at[pl.ds(z * ITEMS, ITEMS)]
    to_lines = [
        send(own_a, own_a, line_send.at[0, d], line_recv.at[0, d], peer)
        for d, peer in enumerate(x_peers)
    ] + [
        send(own_b, own_b, line_send.at[1, d], line_recv.at[1, d], peer)
        for d, peer in enumerate(z_peers)
    ]

    def near_others(stage):
        for copy in to_halo[2 * stage + 2 : 2 * stage + 4] if stage else to_halo[:4]:
            copy.wait_recv()
        end = FIRST + stage * THIRD
        if stage:
            for i in range(THIRD):
                window[LEAVES - end + i] = late[stage - 1, 0, i]
                window[2 * LEAVES + end - THIRD + i] = late[stage - 1, 1, i]
            leaves = [*range(LEAVES - end, LEAVES - end + THIRD), *range(end - THIRD, end)]
        else:
            leaves = range(LEAVES - end, end)
        for leaf in leaves:
            value = total[:, leaf * LEAF : (leaf + 1) * LEAF]
            for k in range(1, NEAR):
                at = place_of(near_list[k, leaf], me * LEAVES - LEAVES, 3 * LEAVES)
                value = value + nt(window[at], block_buf[leaf, k])
            total[:, leaf * LEAF : (leaf + 1) * LEAF] = value

    def spot(node, item):
        branch = node if item else node >> 2
        inside = 8 + (branch & 1) if item else (branch & 1) * 4 + (node & 3)
        return branch >> 3, (branch >> 1) & 3, inside

    for copy in to_choose:
        copy.wait_recv()
    for d in range(6):
        for k in range(SLOTS):
            if k < 4:
                at = spot(jnp.maximum(peer_branches[d, 0, k], 0), True)
            else:
                at = spot(jnp.maximum(peer_nodes[d, s, k - 4], 0), False)
            choice[d * SLOTS + k] = at[0 if d < 3 else 1] * ITEMS + at[2]
    own_choice, absent = [], []
    for k in range(SLOTS):
        partner = branch_pairs[0, k] if k < 4 else node_pairs[s, k - 4]
        own_choice.append(spot(jnp.maximum(partner, 0), k < 4))
        absent.append(partner)

    for part in range(PARTS // 2, PARTS):
        near_self(part)
    for copy in loads[5:]:
        copy.wait()
    for k in range(4):
        coupling_pair[k] = pair_of(branch_coupling_raw[k])
    for k in range(8):
        coupling_pair[4 + k] = pair_of(node_coupling_raw[k])

    for copy in to_mids:
        copy.wait_recv()
    for q in range(MIDS):
        field = jnp.zeros((RHS, 128), f32)
        for k in range(4):
            at = place_of(mid_pairs[k, q], me * MIDS - MIDS, 3 * MIDS)
            field = field + apply_nt(mid_window[at], pair_of(mid_coupling_raw[q, k]))
        mid_field[q] = field

    for stage in range(BESIDE_LINE):
        near_others(stage)

    for copy in to_lines:
        copy.wait_recv()
    to_planes = []
    for d in range(3):
        for k in range(SLOTS):
            chosen_a[d * SLOTS + k] = line_a[choice[(2 - d) * SLOTS + k]]
            chosen_b[d * SLOTS + k] = line_b[choice[(5 - d) * SLOTS + k]]
        at = pl.ds(d * SLOTS, SLOTS)
        to_planes.append(
            send(chosen_a.at[at], got_a.at[pl.ds(z * SLOTS, SLOTS)],
                 plane_send.at[0, d], plane_recv.at[0, d], z_peers[d])
        )
        to_planes.append(
            send(chosen_b.at[at], got_b.at[pl.ds(x * SLOTS, SLOTS)],
                 plane_send.at[1, d], plane_recv.at[1, d], x_peers[d])
        )
    for k in range(SLOTS):
        at_x, at_z, item = own_choice[k]
        got_a[z * SLOTS + k] = line_a[at_x * ITEMS + item]
        got_b[x * SLOTS + k] = line_b[at_z * ITEMS + item]

    for stage in range(BESIDE_LINE, STAGES):
        near_others(stage)

    for copy in to_planes:
        copy.wait_recv()

    def gathered(k):
        at_x, at_z, _ = own_choice[k]
        return jnp.concatenate(
            [
                got_a[place_of(absent[k], absent[k] - (at_z * SLOTS + k), 4 * SLOTS)],
                got_b[place_of(absent[k], absent[k] - (at_x * SLOTS + k), 4 * SLOTS)],
            ],
            axis=0,
        )

    field = jnp.zeros((RHS, 128), f32)
    for k in range(4):
        field = field + apply_nt(gathered(k), coupling_pair[k])
    nodes_field = jnp.zeros((RHS, 128), f32)
    for k in range(4, SLOTS):
        nodes_field = nodes_field + apply_nt(gathered(k), coupling_pair[k])
    field = nodes_field + apply_nt(split(field), transfer_pair[place])
    node_field = split(field)
    for q in range(MIDS):
        mid_window[q] = split(mid_field[q] + apply_nt(node_field, mid_transfer_pair[q]))

    for part in range(PARTS):
        group = range(part * per, part * per + per)
        fields = [split(apply_nt(mid_window[leaf_parent[0, leaf]], up_pair[leaf])) for leaf in group]
        for leaf, field in zip(group, fields):
            own = basis_buf[leaf]
            far = nn(field, jnp.concatenate([own, own], axis=0))
            total[:, leaf * LEAF : (leaf + 1) * LEAF] += far
    for copy in [to_core] + to_column + to_choose + to_mids + to_halo + to_lines + to_planes:
        copy.wait_send()


def on_device(
    right_sides, near_blocks, near_list, leaf_basis, leaf_parent, leaf_upward_matrix, mid_pairs,
    mid_coupling, mid_transfer, node_pairs, node_coupling, node_transfer, branch_pairs,
    branch_coupling,
):
    dma = pltpu.SemaphoreType.DMA
    smem = pl.BlockSpec(memory_space=pltpu.SMEM)
    hbm = pl.BlockSpec(memory_space=pltpu.HBM)
    return pl.pallas_call(
        kernel,
        out_shape=pltpu.VMEM((RHS, COLS), f32),
        in_specs=[smem] * 5 + [hbm] * 9,
        out_specs=pl.BlockSpec(memory_space=pltpu.VMEM),
        scratch_shapes=[
            pltpu.VMEM((RHS, COLS), bf16),
            pltpu.VMEM((3 * LEAVES + 1, RHS, LEAF), bf16),
            pltpu.VMEM((STAGES - 1, 2, THIRD, RHS, LEAF), bf16),
            pltpu.VMEM((LEAVES, NEAR, LEAF, LEAF), bf16),
            pltpu.VMEM((LEAVES, RANK, LEAF), bf16),
            pltpu.VMEM((LEAVES, RANK, RANK), f32),
            pltpu.VMEM((MIDS, 4, RANK, RANK), f32),
            pltpu.VMEM((MIDS, RANK, RANK), f32),
            pltpu.VMEM((8, RANK, RANK), f32),
            pltpu.VMEM((2, 4, RANK, RANK), f32),
            pltpu.VMEM((4, RANK, RANK), f32),
            pltpu.VMEM((LEAVES, RANK, 256), bf16),
            pltpu.VMEM((MIDS, RANK, 256), bf16),
            pltpu.VMEM((8, RANK, 256), bf16),
            pltpu.VMEM((SLOTS, RANK, 256), bf16),
            pltpu.VMEM((LEAVES + 1, RHS, 128), f32),
            pltpu.VMEM((3 * MIDS + 1, RHS, 128), bf16),
            pltpu.VMEM((MIDS, RHS, 128), f32),
            pltpu.VMEM((8, RHS, 128), bf16),
            pltpu.VMEM((4 * ITEMS, 16, 128), bf16),
            pltpu.VMEM((4 * ITEMS, 16, 128), bf16),
            pltpu.VMEM((3 * SLOTS, 16, 128), bf16),
            pltpu.VMEM((3 * SLOTS, 16, 128), bf16),
            pltpu.VMEM((4 * SLOTS + 1, 16, 128), bf16),
            pltpu.VMEM((4 * SLOTS + 1, 16, 128), bf16),
            pltpu.SMEM((6, 4, 8), jnp.int32),
            pltpu.SMEM((6, 1, 4), jnp.int32),
            pltpu.SMEM((6 * SLOTS,), jnp.int32),
            dma((8,)), dma((PARTS,)), dma((2, STAGES + 1)), dma((2, STAGES + 1)), dma((2,)), dma((2,)),
            dma, dma, dma((7,)), dma((7,)), dma((2, 6)), dma((2, 6)), dma((2, 3)), dma((2, 3)), dma((2, 3)), dma((2, 3)),
        ],
        compiler_params=pltpu.CompilerParams(
            collective_id=0, has_side_effects=True, vmem_limit_bytes=58 * 2**20
        ),
        cost_estimate=pl.CostEstimate(
            flops=10**9, bytes_accessed=24 * 10**6, transcendentals=0
        ),
    )(
        near_list.T, leaf_parent, mid_pairs.T, node_pairs, branch_pairs,
        right_sides, near_blocks, leaf_basis, leaf_upward_matrix, mid_coupling, mid_transfer,
        node_coupling, node_transfer, branch_coupling,
    )


def solution(mesh):
    rows = ("branch", "sub")
    return jax.shard_map(
        on_device,
        mesh=mesh,
        in_specs=(
            P(None, rows),
            P(rows, None, None, None),
            P(rows, None),
            P(rows, None, None),
            P(rows, None),
            P(rows, None, None),
            P(rows, None),
            P(rows, None, None, None),
            P(rows, None, None),
            P("branch", None),
            P("branch", None, None, None),
            P("branch", None, None),
            P("branch", None),
            P("branch", None, None, None),
        ),
        out_specs=P(None, rows),
        check_vma=False,
    )
```

```python
import jax
import jax.numpy as jnp
from jax import lax
from jax.experimental import pallas as pl
from jax.experimental.pallas import tpu as pltpu
from jax.sharding import PartitionSpec as P

MESH = pl.DeviceIdType.MESH
f32, bf16 = jnp.float32, jnp.bfloat16
RHS, LEAF, RANK, LEAVES, NEAR, MIDS = 32, 256, 64, 24, 6, 6
COLS = LEAVES * LEAF
PARTS = 4
GROUP = 8
THIRD = 3
STAGES = 4
FIRST = LEAVES - (STAGES - 1) * THIRD
SECOND = 12
BESIDE_LINE = 1
SLOTS = 12
ITEMS = 10


def nn(x, w):
    return lax.dot_general(x, w, (((1,), (0,)), ((), ())), preferred_element_type=f32)


def nt(x, w):
    return lax.dot_general(x, w, (((1,), (1,)), ((), ())), preferred_element_type=f32)


def split(value):
    high = value.astype(bf16).astype(f32)
    lane = lax.broadcasted_iota(jnp.int32, value.shape, 1)
    return jnp.where(lane < RANK, high, value - high).astype(bf16)


def halves(w):
    both = jnp.concatenate([w, w], axis=1)
    high = both.astype(bf16)
    return high, (both - high.astype(f32)).astype(bf16)


def pair_of(w):
    return jnp.concatenate(halves(w), axis=1)


def twice(x):
    return jnp.concatenate([x, x], axis=1)


def apply_nn(x, pair):
    high, low = pair[:, :128], pair[:, 128:]
    return nn(twice(x), jnp.concatenate([high, high, low, low], axis=0))


def apply_nt(x, pair):
    return nt(twice(x), jnp.concatenate([pair, pair], axis=0))


def place_of(partner, base, empty):
    absent = -jnp.minimum(partner, 0)
    at = (partner - base) * (1 - absent) + empty * absent
    return jnp.minimum(jnp.maximum(at, 0), empty)


def kernel(
    near_list, leaf_parent, mid_pairs, node_pairs, branch_pairs,
    rhs, blocks, basis, upward, mid_coupling, mid_transfer, node_coupling, node_transfer,
    branch_coupling, total,
    rhs_buf, window, late, block_buf, basis_buf, up_raw, mid_coupling_raw, mid_transfer_raw,
    node_coupling_raw, transfer_raw, branch_coupling_raw, up_pair, mid_transfer_pair,
    transfer_pair, coupling_pair, raised, mid_window, mid_field, column, line_a, line_b, chosen_a,
    chosen_b, got_a, got_b, peer_nodes, peer_branches, choice,
    load_sem, block_sem, halo_send, halo_recv, mid_send, mid_recv, transfer_send, transfer_recv,
    column_send, column_recv, pair_send, pair_recv, line_send, line_recv, plane_send, plane_recv,
):
    b, s = lax.axis_index("branch"), lax.axis_index("sub")
    core, z, x = b % 2, (b // 2) % 4, b // 8
    me = b * 4 + s
    place = core * 4 + s

    def device(at):
        return (at // 4, at % 4)

    right, left = device((me + 1) % 128), device((me + 127) % 128)
    column_peers = []
    for d in (2, 6, 1, 3, 5, 7, 4):
        at = (place + d) % 8
        column_peers.append((x * 8 + z * 2 + at // 4, at % 4))
    x_peers = [(((x + d) % 4) * 8 + z * 2 + core, s) for d in (1, 2, 3)]
    z_peers = [(x * 8 + ((z + d) % 4) * 2 + core, s) for d in (1, 2, 3)]
    other_core = (x * 8 + z * 2 + 1 - core, s)
    peers = [right, left] + column_peers + x_peers + z_peers

    barrier = pltpu.get_barrier_semaphore()
    for peer in peers:
        pl.semaphore_signal(barrier, inc=1, device_id=peer, device_id_type=MESH)

    def send(src, dst, send_sem, recv_sem, peer):
        copy = pltpu.make_async_remote_copy(
            src_ref=src, dst_ref=dst, send_sem=send_sem, recv_sem=recv_sem,
            device_id=peer, device_id_type=MESH,
        )
        copy.start()
        return copy

    loads = [
        pltpu.make_async_copy(src, dst, load_sem.at[i])
        for i, (src, dst) in enumerate([
            (rhs, rhs_buf),
            (basis, basis_buf),
            (upward, up_raw),
            (mid_transfer, mid_transfer_raw),
            (node_transfer, transfer_raw.at[core]),
            (mid_coupling, mid_coupling_raw),
            (node_coupling.at[s], node_coupling_raw),
            (branch_coupling.at[0], branch_coupling_raw),
        ])
    ]
    per = LEAVES // PARTS
    block_loads = [
        pltpu.make_async_copy(
            blocks.at[pl.ds(i * per, per)], block_buf.at[pl.ds(i * per, per)], block_sem.at[i]
        )
        for i in range(PARTS)
    ]
    for copy in loads[:3]:
        copy.start()
    for leaf in [*range(LEAVES - FIRST), *range(2 * LEAVES + FIRST, 3 * LEAVES + 1)]:
        window[leaf] = jnp.zeros((RHS, LEAF), bf16)
    mid_window[3 * MIDS] = jnp.zeros((RHS, 128), bf16)
    raised[LEAVES] = jnp.zeros((RHS, 128), f32)
    got_a[4 * SLOTS] = jnp.zeros((16, 128), bf16)
    got_b[4 * SLOTS] = jnp.zeros((16, 128), bf16)

    def columns_of(leaf):
        return pl.ds(pl.multiple_of(leaf * LEAF, LEAF), LEAF)

    parents = [leaf_parent[0, leaf] for leaf in range(LEAVES)]
    ends = [0]
    for q in range(1, MIDS):
        below = 0
        for parent in parents:
            below = below + jnp.minimum(jnp.maximum(q - parent, 0), 1)
        ends.append(below)
    ends.append(LEAVES)
    for copy in loads[:3]:
        copy.wait()
    for copy in loads[3:] + block_loads:
        copy.start()
    for leaf in range(LEAVES):
        window[LEAVES + leaf] = rhs_buf[:, leaf * LEAF : (leaf + 1) * LEAF]
    def send_halo(stage):
        if stage < 0:
            size = -stage
            begin = FIRST - size if stage == -SECOND else 0
            end = begin + size
            there = [window.at[pl.ds(LEAVES - end, size)], window.at[pl.ds(2 * LEAVES + begin, size)]]
        else:
            size, end = THIRD, FIRST + (stage + 1) * THIRD
            there = [late.at[stage, 0], late.at[stage, 1]]
        here = [window.at[pl.ds(2 * LEAVES - end, size)], window.at[pl.ds(LEAVES + end - size, size)]]
        slot = stage + 2 if stage >= 0 else (1 if stage == -SECOND else 0)
        return [
            send(here[i], there[i], halo_send.at[i, slot], halo_recv.at[i, slot], peer)
            for i, peer in enumerate((right, left))
        ]


    for first in range(0, LEAVES, GROUP):
        group = range(first, first + GROUP)
        coefs = []
        for leaf in group:
            values = rhs_buf[:, leaf * LEAF : (leaf + 1) * LEAF]
            own = basis_buf[leaf]
            coefs.append(nt(values, jnp.concatenate([own, own], axis=0)))
            up_pair[leaf] = pair_of(up_raw[leaf])
        for leaf, coef in zip(group, coefs):
            raised[leaf] = apply_nn(split(coef), up_pair[leaf])

    pl.semaphore_wait(barrier, len(peers))
    to_halo = send_halo(SECOND - FIRST)

    mids = []
    for q in range(MIDS):
        value = raised[ends[q]]
        for i in range(1, 6):
            leaf = ends[q] + i
            past = jnp.minimum(jnp.maximum(leaf + 1 - ends[q + 1], 0), 1)
            value = value + raised[leaf * (1 - past) + LEAVES * past]
        mids.append(value)
    loads[3].wait()
    node = jnp.zeros((RHS, 128), f32)
    for q in range(MIDS):
        pair = jnp.concatenate(halves(mid_transfer_raw[q]), axis=1)
        mid_transfer_pair[q] = pair
        coef = split(mids[q])
        mid_window[MIDS + q] = coef
        node = node + apply_nn(coef, pair)
    column[place] = split(node)

    to_column = [
        send(column.at[place], column.at[place], column_send.at[d], column_recv.at[d], peer)
        for d, peer in enumerate(column_peers)
    ]
    loads[4].wait()
    to_core = send(
        transfer_raw.at[core], transfer_raw.at[core], transfer_send, transfer_recv, other_core
    )
    to_choose = []
    for d, peer in enumerate(z_peers + x_peers):
        to_choose.append(
            send(node_pairs, peer_nodes.at[d], pair_send.at[0, d], pair_recv.at[0, d], peer)
        )
        to_choose.append(
            send(branch_pairs, peer_branches.at[d], pair_send.at[1, d], pair_recv.at[1, d], peer)
        )

    own_mids = mid_window.at[pl.ds(MIDS, MIDS)]
    to_mids = [
        send(own_mids, mid_window.at[pl.ds(0, MIDS)], mid_send.at[0], mid_recv.at[0], right),
        send(own_mids, mid_window.at[pl.ds(2 * MIDS, MIDS)], mid_send.at[1], mid_recv.at[1], left),
    ]
    to_halo += send_halo(-SECOND)

    def near_self(part):
        block_loads[part].wait()
        for leaf in range(part * per, part * per + per):
            total[:, leaf * LEAF : (leaf + 1) * LEAF] = nt(
                rhs_buf[:, leaf * LEAF : (leaf + 1) * LEAF], block_buf[leaf, 0]
            )

    for sub in range(4):
        transfer_pair[core * 4 + sub] = pair_of(transfer_raw[core, sub])
    for part in range(PARTS // 2):
        near_self(part)

    to_core.wait_recv()
    for sub in range(4):
        transfer_pair[(1 - core) * 4 + sub] = pair_of(transfer_raw[1 - core, sub])
    for copy in to_column:
        copy.wait_recv()
    for stage in range(STAGES - 1):
        to_halo += send_halo(stage)
    for half in range(2):
        top = jnp.zeros((RHS, 128), f32)
        for sub in range(4):
            item = half * 4 + sub
            top = top + apply_nn(column[item], transfer_pair[item])
        top = split(top)
        line_a[x * ITEMS + 8 + half] = top[:16]
        line_b[z * ITEMS + 8 + half] = top[16:]
    for item in range(8):
        value = column[item]
        line_a[x * ITEMS + item] = value[:16]
        line_b[z * ITEMS + item] = value[16:]
    own_a, own_b = line_a.at[pl.ds(x * ITEMS, ITEMS)], line_b.at[pl.ds(z * ITEMS, ITEMS)]
    to_lines = []
    for d in (1, 0, 2):
        to_lines.append(
            send(own_a, own_a, line_send.at[0, d], line_recv.at[0, d], x_peers[d])
        )
        to_lines.append(
            send(own_b, own_b, line_send.at[1, d], line_recv.at[1, d], z_peers[d])
        )

    def near_others(stage):
        for copy in to_halo[2 * stage + 2 : 2 * stage + 4] if stage else to_halo[:4]:
            copy.wait_recv()
        end = FIRST + stage * THIRD
        if stage:
            for i in range(THIRD):
                window[LEAVES - end + i] = late[stage - 1, 0, i]
                window[2 * LEAVES + end - THIRD + i] = late[stage - 1, 1, i]
            leaves = [*range(LEAVES - end, LEAVES - end + THIRD), *range(end - THIRD, end)]
        else:
            leaves = range(LEAVES - end, end)
        for leaf in leaves:
            value = total[:, leaf * LEAF : (leaf + 1) * LEAF]
            for k in range(1, NEAR):
                at = place_of(near_list[k, leaf], me * LEAVES - LEAVES, 3 * LEAVES)
                value = value + nt(window[at], block_buf[leaf, k])
            total[:, leaf * LEAF : (leaf + 1) * LEAF] = value

    def spot(node, item):
        branch = node if item else node >> 2
        inside = 8 + (branch & 1) if item else (branch & 1) * 4 + (node & 3)
        return branch >> 3, (branch >> 1) & 3, inside

    for copy in to_choose:
        copy.wait_recv()
    for d in range(6):
        for k in range(SLOTS):
            if k < 4:
                at = spot(jnp.maximum(peer_branches[d, 0, k], 0), True)
            else:
                at = spot(jnp.maximum(peer_nodes[d, s, k - 4], 0), False)
            choice[d * SLOTS + k] = at[0 if d < 3 else 1] * ITEMS + at[2]
    own_choice, absent = [], []
    for k in range(SLOTS):
        partner = branch_pairs[0, k] if k < 4 else node_pairs[s, k - 4]
        own_choice.append(spot(jnp.maximum(partner, 0), k < 4))
        absent.append(partner)

    for part in range(PARTS // 2, PARTS):
        near_self(part)
    for copy in loads[5:]:
        copy.wait()
    for k in range(4):
        coupling_pair[k] = pair_of(branch_coupling_raw[k])
    for k in range(8):
        coupling_pair[4 + k] = pair_of(node_coupling_raw[k])

    for copy in to_mids:
        copy.wait_recv()
    for q in range(MIDS):
        field = jnp.zeros((RHS, 128), f32)
        for k in range(4):
            at = place_of(mid_pairs[k, q], me * MIDS - MIDS, 3 * MIDS)
            field = field + apply_nt(mid_window[at], pair_of(mid_coupling_raw[q, k]))
        mid_field[q] = field

    for stage in range(BESIDE_LINE):
        near_others(stage)

    for copy in to_lines:
        copy.wait_recv()
    to_planes = []
    for d in (1, 0, 2):
        for k in range(SLOTS):
            chosen_a[d * SLOTS + k] = line_a[choice[(2 - d) * SLOTS + k]]
            chosen_b[d * SLOTS + k] = line_b[choice[(5 - d) * SLOTS + k]]
        at = pl.ds(d * SLOTS, SLOTS)
        to_planes.append(
            send(chosen_a.at[at], got_a.at[pl.ds(z * SLOTS, SLOTS)],
                 plane_send.at[0, d], plane_recv.at[0, d], z_peers[d])
        )
        to_planes.append(
            send(chosen_b.at[at], got_b.at[pl.ds(x * SLOTS, SLOTS)],
                 plane_send.at[1, d], plane_recv.at[1, d], x_peers[d])
        )
    for k in range(SLOTS):
        at_x, at_z, item = own_choice[k]
        got_a[z * SLOTS + k] = line_a[at_x * ITEMS + item]
        got_b[x * SLOTS + k] = line_b[at_z * ITEMS + item]

    for stage in range(BESIDE_LINE, STAGES):
        near_others(stage)

    for copy in to_planes:
        copy.wait_recv()

    def gathered(k):
        at_x, at_z, _ = own_choice[k]
        return jnp.concatenate(
            [
                got_a[place_of(absent[k], absent[k] - (at_z * SLOTS + k), 4 * SLOTS)],
                got_b[place_of(absent[k], absent[k] - (at_x * SLOTS + k), 4 * SLOTS)],
            ],
            axis=0,
        )

    field = jnp.zeros((RHS, 128), f32)
    for k in range(4):
        field = field + apply_nt(gathered(k), coupling_pair[k])
    nodes_field = jnp.zeros((RHS, 128), f32)
    for k in range(4, SLOTS):
        nodes_field = nodes_field + apply_nt(gathered(k), coupling_pair[k])
    field = nodes_field + apply_nt(split(field), transfer_pair[place])
    node_field = split(field)
    for q in range(MIDS):
        mid_window[q] = split(mid_field[q] + apply_nt(node_field, mid_transfer_pair[q]))

    for part in range(PARTS):
        group = range(part * per, part * per + per)
        fields = [split(apply_nt(mid_window[leaf_parent[0, leaf]], up_pair[leaf])) for leaf in group]
        for leaf, field in zip(group, fields):
            own = basis_buf[leaf]
            far = nn(field, jnp.concatenate([own, own], axis=0))
            total[:, leaf * LEAF : (leaf + 1) * LEAF] += far
    for copy in [to_core] + to_column + to_choose + to_mids + to_halo + to_lines + to_planes:
        copy.wait_send()


def on_device(
    right_sides, near_blocks, near_list, leaf_basis, leaf_parent, leaf_upward_matrix, mid_pairs,
    mid_coupling, mid_transfer, node_pairs, node_coupling, node_transfer, branch_pairs,
    branch_coupling,
):
    dma = pltpu.SemaphoreType.DMA
    smem = pl.BlockSpec(memory_space=pltpu.SMEM)
    hbm = pl.BlockSpec(memory_space=pltpu.HBM)
    return pl.pallas_call(
        kernel,
        out_shape=pltpu.VMEM((RHS, COLS), f32),
        in_specs=[smem] * 5 + [hbm] * 9,
        out_specs=pl.BlockSpec(memory_space=pltpu.VMEM),
        scratch_shapes=[
            pltpu.VMEM((RHS, COLS), bf16),
            pltpu.VMEM((3 * LEAVES + 1, RHS, LEAF), bf16),
            pltpu.VMEM((STAGES - 1, 2, THIRD, RHS, LEAF), bf16),
            pltpu.VMEM((LEAVES, NEAR, LEAF, LEAF), bf16),
            pltpu.VMEM((LEAVES, RANK, LEAF), bf16),
            pltpu.VMEM((LEAVES, RANK, RANK), f32),
            pltpu.VMEM((MIDS, 4, RANK, RANK), f32),
            pltpu.VMEM((MIDS, RANK, RANK), f32),
            pltpu.VMEM((8, RANK, RANK), f32),
            pltpu.VMEM((2, 4, RANK, RANK), f32),
            pltpu.VMEM((4, RANK, RANK), f32),
            pltpu.VMEM((LEAVES, RANK, 256), bf16),
            pltpu.VMEM((MIDS, RANK, 256), bf16),
            pltpu.VMEM((8, RANK, 256), bf16),
            pltpu.VMEM((SLOTS, RANK, 256), bf16),
            pltpu.VMEM((LEAVES + 1, RHS, 128), f32),
            pltpu.VMEM((3 * MIDS + 1, RHS, 128), bf16),
            pltpu.VMEM((MIDS, RHS, 128), f32),
            pltpu.VMEM((8, RHS, 128), bf16),
            pltpu.VMEM((4 * ITEMS, 16, 128), bf16),
            pltpu.VMEM((4 * ITEMS, 16, 128), bf16),
            pltpu.VMEM((3 * SLOTS, 16, 128), bf16),
            pltpu.VMEM((3 * SLOTS, 16, 128), bf16),
            pltpu.VMEM((4 * SLOTS + 1, 16, 128), bf16),
            pltpu.VMEM((4 * SLOTS + 1, 16, 128), bf16),
            pltpu.SMEM((6, 4, 8), jnp.int32),
            pltpu.SMEM((6, 1, 4), jnp.int32),
            pltpu.SMEM((6 * SLOTS,), jnp.int32),
            dma((8,)), dma((PARTS,)), dma((2, STAGES + 1)), dma((2, STAGES + 1)), dma((2,)), dma((2,)),
            dma, dma, dma((7,)), dma((7,)), dma((2, 6)), dma((2, 6)), dma((2, 3)), dma((2, 3)), dma((2, 3)), dma((2, 3)),
        ],
        compiler_params=pltpu.CompilerParams(
            collective_id=0, has_side_effects=True, vmem_limit_bytes=58 * 2**20
        ),
        cost_estimate=pl.CostEstimate(
            flops=10**9, bytes_accessed=24 * 10**6, transcendentals=0
        ),
    )(
        near_list.T, leaf_parent, mid_pairs.T, node_pairs, branch_pairs,
        right_sides, near_blocks, leaf_basis, leaf_upward_matrix, mid_coupling, mid_transfer,
        node_coupling, node_transfer, branch_coupling,
    )


def solution(mesh):
    rows = ("branch", "sub")
    return jax.shard_map(
        on_device,
        mesh=mesh,
        in_specs=(
            P(None, rows),
            P(rows, None, None, None),
            P(rows, None),
            P(rows, None, None),
            P(rows, None),
            P(rows, None, None),
            P(rows, None),
            P(rows, None, None, None),
            P(rows, None, None),
            P("branch", None),
            P("branch", None, None, None),
            P("branch", None, None),
            P("branch", None),
            P("branch", None, None, None),
        ),
        out_specs=P(None, rows),
        check_vma=False,
    )
```

```python
import jax
import jax.numpy as jnp
from jax import lax
from jax.experimental import pallas as pl
from jax.experimental.pallas import tpu as pltpu
from jax.sharding import PartitionSpec as P

MESH = pl.DeviceIdType.MESH
f32, bf16 = jnp.float32, jnp.bfloat16
RHS, LEAF, RANK, LEAVES, NEAR, MIDS = 32, 256, 64, 24, 6, 6
COLS = LEAVES * LEAF
PARTS = 4
GROUP = 8
THIRD = 3
STAGES = 4
FIRST = LEAVES - (STAGES - 1) * THIRD
SECOND = 12
BESIDE_LINE = 1
SLOTS = 12
ITEMS = 10


def nn(x, w):
    return lax.dot_general(x, w, (((1,), (0,)), ((), ())), preferred_element_type=f32)


def nt(x, w):
    return lax.dot_general(x, w, (((1,), (1,)), ((), ())), preferred_element_type=f32)


def split(value):
    high = value.astype(bf16).astype(f32)
    lane = lax.broadcasted_iota(jnp.int32, value.shape, 1)
    return jnp.where(lane < RANK, high, value - high).astype(bf16)


def halves(w):
    both = jnp.concatenate([w, w], axis=1)
    high = both.astype(bf16)
    return high, (both - high.astype(f32)).astype(bf16)


def pair_of(w):
    return jnp.concatenate(halves(w), axis=1)


def twice(x):
    return jnp.concatenate([x, x], axis=1)


def apply_nn(x, pair):
    high, low = pair[:, :128], pair[:, 128:]
    return nn(twice(x), jnp.concatenate([high, high, low, low], axis=0))


def apply_nt(x, pair):
    return nt(twice(x), jnp.concatenate([pair, pair], axis=0))


def place_of(partner, base, empty):
    absent = -jnp.minimum(partner, 0)
    at = (partner - base) * (1 - absent) + empty * absent
    return jnp.minimum(jnp.maximum(at, 0), empty)


def kernel(
    near_list, leaf_parent, mid_pairs, node_pairs, branch_pairs,
    rhs, blocks, basis, upward, mid_coupling, mid_transfer, node_coupling, node_transfer,
    branch_coupling, total,
    rhs_buf, window, late, block_buf, basis_buf, up_raw, mid_coupling_raw, mid_transfer_raw,
    node_coupling_raw, transfer_raw, branch_coupling_raw, up_pair, mid_transfer_pair,
    transfer_pair, coupling_pair, raised, mid_window, mid_field, column, line_a, line_b, chosen_a,
    chosen_b, got_a, got_b, peer_nodes, peer_branches, choice,
    load_sem, block_sem, halo_send, halo_recv, mid_send, mid_recv, transfer_send, transfer_recv,
    column_send, column_recv, pair_send, pair_recv, line_send, line_recv, plane_send, plane_recv,
):
    b, s = lax.axis_index("branch"), lax.axis_index("sub")
    core, z, x = b % 2, (b // 2) % 4, b // 8
    me = b * 4 + s
    place = core * 4 + s

    def device(at):
        return (at // 4, at % 4)

    right, left = device((me + 1) % 128), device((me + 127) % 128)
    column_peers = []
    for d in (2, 6, 1, 3, 5, 7, 4):
        at = (place + d) % 8
        column_peers.append((x * 8 + z * 2 + at // 4, at % 4))
    x_peers = [(((x + d) % 4) * 8 + z * 2 + core, s) for d in (1, 2, 3)]
    z_peers = [(x * 8 + ((z + d) % 4) * 2 + core, s) for d in (1, 2, 3)]
    other_core = (x * 8 + z * 2 + 1 - core, s)
    peers = [right, left] + column_peers + x_peers + z_peers

    barrier = pltpu.get_barrier_semaphore()
    for peer in peers:
        pl.semaphore_signal(barrier, inc=1, device_id=peer, device_id_type=MESH)

    def send(src, dst, send_sem, recv_sem, peer):
        copy = pltpu.make_async_remote_copy(
            src_ref=src, dst_ref=dst, send_sem=send_sem, recv_sem=recv_sem,
            device_id=peer, device_id_type=MESH,
        )
        copy.start()
        return copy

    loads = [
        pltpu.make_async_copy(src, dst, load_sem.at[i])
        for i, (src, dst) in enumerate([
            (rhs, rhs_buf),
            (basis, basis_buf),
            (upward, up_raw),
            (mid_transfer, mid_transfer_raw),
            (node_transfer, transfer_raw.at[core]),
            (mid_coupling, mid_coupling_raw),
            (node_coupling.at[s], node_coupling_raw),
            (branch_coupling.at[0], branch_coupling_raw),
        ])
    ]
    per = LEAVES // PARTS
    block_loads = [
        pltpu.make_async_copy(
            blocks.at[pl.ds(i * per, per)], block_buf.at[pl.ds(i * per, per)], block_sem.at[i]
        )
        for i in range(PARTS)
    ]
    for copy in loads[:3]:
        copy.start()
    for leaf in [*range(LEAVES - FIRST), *range(2 * LEAVES + FIRST, 3 * LEAVES + 1)]:
        window[leaf] = jnp.zeros((RHS, LEAF), bf16)
    mid_window[3 * MIDS] = jnp.zeros((RHS, 128), bf16)
    raised[LEAVES] = jnp.zeros((RHS, 128), f32)
    got_a[4 * SLOTS] = jnp.zeros((16, 128), bf16)
    got_b[4 * SLOTS] = jnp.zeros((16, 128), bf16)

    def columns_of(leaf):
        return pl.ds(pl.multiple_of(leaf * LEAF, LEAF), LEAF)

    parents = [leaf_parent[0, leaf] for leaf in range(LEAVES)]
    ends = [0]
    for q in range(1, MIDS):
        below = 0
        for parent in parents:
            below = below + jnp.minimum(jnp.maximum(q - parent, 0), 1)
        ends.append(below)
    ends.append(LEAVES)
    for copy in loads[:3]:
        copy.wait()
    for copy in loads[3:] + block_loads:
        copy.start()
    for leaf in range(LEAVES):
        window[LEAVES + leaf] = rhs_buf[:, leaf * LEAF : (leaf + 1) * LEAF]
    def send_halo(stage):
        if stage < 0:
            size = -stage
            begin = FIRST - size if stage == -SECOND else 0
            end = begin + size
            there = [window.at[pl.ds(LEAVES - end, size)], window.at[pl.ds(2 * LEAVES + begin, size)]]
        else:
            size, end = THIRD, FIRST + (stage + 1) * THIRD
            there = [late.at[stage, 0], late.at[stage, 1]]
        here = [window.at[pl.ds(2 * LEAVES - end, size)], window.at[pl.ds(LEAVES + end - size, size)]]
        slot = stage + 2 if stage >= 0 else (1 if stage == -SECOND else 0)
        return [
            send(here[i], there[i], halo_send.at[i, slot], halo_recv.at[i, slot], peer)
            for i, peer in enumerate((right, left))
        ]


    for first in range(0, LEAVES, GROUP):
        group = range(first, first + GROUP)
        coefs = []
        for leaf in group:
            values = rhs_buf[:, leaf * LEAF : (leaf + 1) * LEAF]
            own = basis_buf[leaf]
            coefs.append(nt(values, jnp.concatenate([own, own], axis=0)))
            up_pair[leaf] = pair_of(up_raw[leaf])
        for leaf, coef in zip(group, coefs):
            raised[leaf] = apply_nn(split(coef), up_pair[leaf])

    pl.semaphore_wait(barrier, len(peers))
    to_halo = send_halo(SECOND - FIRST)

    mids = []
    for q in range(MIDS):
        value = raised[ends[q]]
        for i in range(1, 6):
            leaf = ends[q] + i
            past = jnp.minimum(jnp.maximum(leaf + 1 - ends[q + 1], 0), 1)
            value = value + raised[leaf * (1 - past) + LEAVES * past]
        mids.append(value)
    loads[3].wait()
    node = jnp.zeros((RHS, 128), f32)
    for q in range(MIDS):
        pair = jnp.concatenate(halves(mid_transfer_raw[q]), axis=1)
        mid_transfer_pair[q] = pair
        coef = split(mids[q])
        mid_window[MIDS + q] = coef
        node = node + apply_nn(coef, pair)
    column[place] = split(node)

    to_column = [
        send(column.at[place], column.at[place], column_send.at[d], column_recv.at[d], peer)
        for d, peer in enumerate(column_peers)
    ]
    loads[4].wait()
    to_core = send(
        transfer_raw.at[core], transfer_raw.at[core], transfer_send, transfer_recv, other_core
    )
    to_choose = []
    for d, peer in enumerate(z_peers + x_peers):
        to_choose.append(
            send(node_pairs, peer_nodes.at[d], pair_send.at[0, d], pair_recv.at[0, d], peer)
        )
        to_choose.append(
            send(branch_pairs, peer_branches.at[d], pair_send.at[1, d], pair_recv.at[1, d], peer)
        )

    own_mids = mid_window.at[pl.ds(MIDS, MIDS)]
    to_mids = [
        send(own_mids, mid_window.at[pl.ds(0, MIDS)], mid_send.at[0], mid_recv.at[0], right),
        send(own_mids, mid_window.at[pl.ds(2 * MIDS, MIDS)], mid_send.at[1], mid_recv.at[1], left),
    ]
    to_halo += send_halo(-SECOND)

    def near_self(part):
        block_loads[part].wait()
        for leaf in range(part * per, part * per + per):
            total[:, leaf * LEAF : (leaf + 1) * LEAF] = nt(
                rhs_buf[:, leaf * LEAF : (leaf + 1) * LEAF], block_buf[leaf, 0]
            )

    for sub in range(4):
        transfer_pair[core * 4 + sub] = pair_of(transfer_raw[core, sub])
    for part in range(PARTS // 2):
        near_self(part)

    to_core.wait_recv()
    for sub in range(4):
        transfer_pair[(1 - core) * 4 + sub] = pair_of(transfer_raw[1 - core, sub])
    for copy in to_column:
        copy.wait_recv()
    for stage in range(STAGES - 1):
        to_halo += send_halo(stage)
    for half in range(2):
        top = jnp.zeros((RHS, 128), f32)
        for sub in range(4):
            item = half * 4 + sub
            top = top + apply_nn(column[item], transfer_pair[item])
        top = split(top)
        line_a[x * ITEMS + 8 + half] = top[:16]
        line_b[z * ITEMS + 8 + half] = top[16:]
    for item in range(8):
        value = column[item]
        line_a[x * ITEMS + item] = value[:16]
        line_b[z * ITEMS + item] = value[16:]
    own_a, own_b = line_a.at[pl.ds(x * ITEMS, ITEMS)], line_b.at[pl.ds(z * ITEMS, ITEMS)]
    to_lines = []
    for d in (1, 0, 2):
        to_lines.append(
            send(own_a, own_a, line_send.at[0, d], line_recv.at[0, d], x_peers[d])
        )
        to_lines.append(
            send(own_b, own_b, line_send.at[1, d], line_recv.at[1, d], z_peers[d])
        )

    def near_others(stage):
        for copy in to_halo[2 * stage + 2 : 2 * stage + 4] if stage else to_halo[:4]:
            copy.wait_recv()
        end = FIRST + stage * THIRD
        if stage:
            for i in range(THIRD):
                window[LEAVES - end + i] = late[stage - 1, 0, i]
                window[2 * LEAVES + end - THIRD + i] = late[stage - 1, 1, i]
            leaves = [*range(LEAVES - end, LEAVES - end + THIRD), *range(end - THIRD, end)]
        else:
            leaves = range(LEAVES - end, end)
        for leaf in leaves:
            value = total[:, leaf * LEAF : (leaf + 1) * LEAF]
            for k in range(1, NEAR):
                at = place_of(near_list[k, leaf], me * LEAVES - LEAVES, 3 * LEAVES)
                value = value + nt(window[at], block_buf[leaf, k])
            total[:, leaf * LEAF : (leaf + 1) * LEAF] = value

    def spot(node, item):
        branch = node if item else node >> 2
        inside = 8 + (branch & 1) if item else (branch & 1) * 4 + (node & 3)
        return branch >> 3, (branch >> 1) & 3, inside

    for copy in to_choose:
        copy.wait_recv()
    for d in range(6):
        for k in range(SLOTS):
            if k < 4:
                at = spot(jnp.maximum(peer_branches[d, 0, k], 0), True)
            else:
                at = spot(jnp.maximum(peer_nodes[d, s, k - 4], 0), False)
            choice[d * SLOTS + k] = at[0 if d < 3 else 1] * ITEMS + at[2]
    own_choice, absent = [], []
    for k in range(SLOTS):
        partner = branch_pairs[0, k] if k < 4 else node_pairs[s, k - 4]
        own_choice.append(spot(jnp.maximum(partner, 0), k < 4))
        absent.append(partner)

    for part in range(PARTS // 2, PARTS):
        near_self(part)
    for copy in loads[5:]:
        copy.wait()
    for k in range(4):
        coupling_pair[k] = pair_of(branch_coupling_raw[k])
    for k in range(8):
        coupling_pair[4 + k] = pair_of(node_coupling_raw[k])

    for copy in to_mids:
        copy.wait_recv()
    for q in range(MIDS):
        field = jnp.zeros((RHS, 128), f32)
        for k in range(4):
            at = place_of(mid_pairs[k, q], me * MIDS - MIDS, 3 * MIDS)
            field = field + apply_nt(mid_window[at], pair_of(mid_coupling_raw[q, k]))
        mid_field[q] = field

    for stage in range(BESIDE_LINE):
        near_others(stage)

    to_planes = []
    for copy in to_lines[0::2]:
        copy.wait_recv()
    for d in (1, 0, 2):
        for k in range(SLOTS):
            chosen_a[d * SLOTS + k] = line_a[choice[(2 - d) * SLOTS + k]]
        to_planes.append(
            send(chosen_a.at[pl.ds(d * SLOTS, SLOTS)], got_a.at[pl.ds(z * SLOTS, SLOTS)],
                 plane_send.at[0, d], plane_recv.at[0, d], z_peers[d])
        )
    for copy in to_lines[1::2]:
        copy.wait_recv()
    for d in (1, 0, 2):
        for k in range(SLOTS):
            chosen_b[d * SLOTS + k] = line_b[choice[(5 - d) * SLOTS + k]]
        to_planes.append(
            send(chosen_b.at[pl.ds(d * SLOTS, SLOTS)], got_b.at[pl.ds(x * SLOTS, SLOTS)],
                 plane_send.at[1, d], plane_recv.at[1, d], x_peers[d])
        )
    for k in range(SLOTS):
        at_x, at_z, item = own_choice[k]
        got_a[z * SLOTS + k] = line_a[at_x * ITEMS + item]
        got_b[x * SLOTS + k] = line_b[at_z * ITEMS + item]

    for stage in range(BESIDE_LINE, STAGES):
        near_others(stage)

    for copy in to_planes:
        copy.wait_recv()

    def gathered(k):
        at_x, at_z, _ = own_choice[k]
        return jnp.concatenate(
            [
                got_a[place_of(absent[k], absent[k] - (at_z * SLOTS + k), 4 * SLOTS)],
                got_b[place_of(absent[k], absent[k] - (at_x * SLOTS + k), 4 * SLOTS)],
            ],
            axis=0,
        )

    field = jnp.zeros((RHS, 128), f32)
    for k in range(4):
        field = field + apply_nt(gathered(k), coupling_pair[k])
    nodes_field = jnp.zeros((RHS, 128), f32)
    for k in range(4, SLOTS):
        nodes_field = nodes_field + apply_nt(gathered(k), coupling_pair[k])
    field = nodes_field + apply_nt(split(field), transfer_pair[place])
    node_field = split(field)
    for q in range(MIDS):
        mid_window[q] = split(mid_field[q] + apply_nt(node_field, mid_transfer_pair[q]))

    for part in range(PARTS):
        group = range(part * per, part * per + per)
        fields = [split(apply_nt(mid_window[leaf_parent[0, leaf]], up_pair[leaf])) for leaf in group]
        for leaf, field in zip(group, fields):
            own = basis_buf[leaf]
            far = nn(field, jnp.concatenate([own, own], axis=0))
            total[:, leaf * LEAF : (leaf + 1) * LEAF] += far
    for copy in [to_core] + to_column + to_choose + to_mids + to_halo + to_lines + to_planes:
        copy.wait_send()


def on_device(
    right_sides, near_blocks, near_list, leaf_basis, leaf_parent, leaf_upward_matrix, mid_pairs,
    mid_coupling, mid_transfer, node_pairs, node_coupling, node_transfer, branch_pairs,
    branch_coupling,
):
    dma = pltpu.SemaphoreType.DMA
    smem = pl.BlockSpec(memory_space=pltpu.SMEM)
    hbm = pl.BlockSpec(memory_space=pltpu.HBM)
    return pl.pallas_call(
        kernel,
        out_shape=pltpu.VMEM((RHS, COLS), f32),
        in_specs=[smem] * 5 + [hbm] * 9,
        out_specs=pl.BlockSpec(memory_space=pltpu.VMEM),
        scratch_shapes=[
            pltpu.VMEM((RHS, COLS), bf16),
            pltpu.VMEM((3 * LEAVES + 1, RHS, LEAF), bf16),
            pltpu.VMEM((STAGES - 1, 2, THIRD, RHS, LEAF), bf16),
            pltpu.VMEM((LEAVES, NEAR, LEAF, LEAF), bf16),
            pltpu.VMEM((LEAVES, RANK, LEAF), bf16),
            pltpu.VMEM((LEAVES, RANK, RANK), f32),
            pltpu.VMEM((MIDS, 4, RANK, RANK), f32),
            pltpu.VMEM((MIDS, RANK, RANK), f32),
            pltpu.VMEM((8, RANK, RANK), f32),
            pltpu.VMEM((2, 4, RANK, RANK), f32),
            pltpu.VMEM((4, RANK, RANK), f32),
            pltpu.VMEM((LEAVES, RANK, 256), bf16),
            pltpu.VMEM((MIDS, RANK, 256), bf16),
            pltpu.VMEM((8, RANK, 256), bf16),
            pltpu.VMEM((SLOTS, RANK, 256), bf16),
            pltpu.VMEM((LEAVES + 1, RHS, 128), f32),
            pltpu.VMEM((3 * MIDS + 1, RHS, 128), bf16),
            pltpu.VMEM((MIDS, RHS, 128), f32),
            pltpu.VMEM((8, RHS, 128), bf16),
            pltpu.VMEM((4 * ITEMS, 16, 128), bf16),
            pltpu.VMEM((4 * ITEMS, 16, 128), bf16),
            pltpu.VMEM((3 * SLOTS, 16, 128), bf16),
            pltpu.VMEM((3 * SLOTS, 16, 128), bf16),
            pltpu.VMEM((4 * SLOTS + 1, 16, 128), bf16),
            pltpu.VMEM((4 * SLOTS + 1, 16, 128), bf16),
            pltpu.SMEM((6, 4, 8), jnp.int32),
            pltpu.SMEM((6, 1, 4), jnp.int32),
            pltpu.SMEM((6 * SLOTS,), jnp.int32),
            dma((8,)), dma((PARTS,)), dma((2, STAGES + 1)), dma((2, STAGES + 1)), dma((2,)), dma((2,)),
            dma, dma, dma((7,)), dma((7,)), dma((2, 6)), dma((2, 6)), dma((2, 3)), dma((2, 3)), dma((2, 3)), dma((2, 3)),
        ],
        compiler_params=pltpu.CompilerParams(
            collective_id=0, has_side_effects=True, vmem_limit_bytes=58 * 2**20
        ),
        cost_estimate=pl.CostEstimate(
            flops=10**9, bytes_accessed=24 * 10**6, transcendentals=0
        ),
    )(
        near_list.T, leaf_parent, mid_pairs.T, node_pairs, branch_pairs,
        right_sides, near_blocks, leaf_basis, leaf_upward_matrix, mid_coupling, mid_transfer,
        node_coupling, node_transfer, branch_coupling,
    )


def solution(mesh):
    rows = ("branch", "sub")
    return jax.shard_map(
        on_device,
        mesh=mesh,
        in_specs=(
            P(None, rows),
            P(rows, None, None, None),
            P(rows, None),
            P(rows, None, None),
            P(rows, None),
            P(rows, None, None),
            P(rows, None),
            P(rows, None, None, None),
            P(rows, None, None),
            P("branch", None),
            P("branch", None, None, None),
            P("branch", None, None),
            P("branch", None),
            P("branch", None, None, None),
        ),
        out_specs=P(None, rows),
        check_vma=False,
    )
```
